256 devices in a mesh: gz: 16 (over z, core), gy: 8 (over y, x_hi), orb: 2 (over x_lo).
Axes of the slice: x: 4 (x_hi: 2, x_lo: 2; x = x_hi * 2 + x_lo), y: 4, z: 8, core: 2. Of those that a mesh axis runs over, the one named last changes fastest.
Arguments:
- orbitals: bfloat16 [4096, 24, 576], P(('gz', 'gy', 'orb')), may hold values from -6 to 6
- occupation: float32 [4096], P(('gz', 'gy', 'orb')), may hold values from 0.5 to 2
- corners: int32 [4096, 3], P(('gz', 'gy', 'orb')), may hold values from 0 to 383, as said below
- kernel_widths: float32 [8], replicated, may hold values from 0.7 to 2.5
- w_in: float32 [8, 64], replicated, may hold values from -2 to 2
- b_in: float32 [64], replicated, may hold values from -3 to 3
- w_mid: float32 [64, 64], replicated, may hold values from -0.75 to 0.75
- b_mid: float32 [64], replicated, may hold values from -3 to 3
- w_out: float32 [64], replicated, may hold values from -0.75 to 0.75
- b_out: float32 [1], replicated, may hold values from -3 to 3
Outputs:
- potential: bfloat16 [384, 192, 128], P('gz', 'gy')
- applied: bfloat16 [4096, 24, 576], P(('gz', 'gy', 'orb'))
The draws below stay inside these ranges and needn't reach their ends.
Inputs may be any that keep to these rules, and one draw needn't show every extreme that they name: Orbital i is held by device i // 16 of the axes gz, gy, orb taken together. Its row corners[i,1] lies in the 24 rows of that device's gy index. Among the 16 orbitals of one device, at most 2 have their plane corners[i,0] in the same slab of 24 planes, and on every device some slab holds exactly 2 of them. Columns lie in 0 to 127, rows in 0 to 191, planes in 0 to 383; the first and the last plane are taken in every draw.
All inputs are finite; a program needn't handle non-finite values.
Results may differ from the reference program's by a relative error of at most 0.0055.
Values may be sent and summed in bfloat16 or wider, within the bound.
No kernel may reach another device: no remote copies, remote signals or barrier semaphores. Data moves between devices by JAX's collectives and lax.ppermute only.
A program may use at most 64 MiB of HBM per device.

```python
import math
import jax
import jax.numpy as jnp
from jax import lax

BOX = 24
CHAN = 8
HID = 64
RAD = 6
CZ = 24
CY = 24
NX = 128
CAP = 2
CELL_BLOCK = 12288
B_DEV = 16
NZ = 384
NY = 192
NORB = 4096


def shuffled_row(subkey):
    return jax.random.permutation(subkey, CAP * (NZ // CZ))


def mixed_row(subkey):
    return jax.random.permutation(subkey, B_DEV)


def draw_corners(key, part):
    slab_count = NZ // CZ
    row_count = NY // CY
    device_count = NORB // B_DEV
    owner_count = device_count // (slab_count * row_count)
    column_count = row_count * owner_count
    device_ids = jnp.arange(device_count, dtype=jnp.int32)
    column = device_ids % column_count
    favored = jax.random.randint(jax.random.fold_in(key, 11), (column_count,), 0, slab_count)
    favored = favored.at[0].set(slab_count - 1).at[1].set(0)
    entries = jnp.arange(CAP * slab_count, dtype=jnp.int32) % slab_count
    shuffled = jax.vmap(shuffled_row)(jax.random.split(jax.random.fold_in(key, 12), device_count))
    priority = jnp.where(entries[None, :] == 0, -1, shuffled.astype(jnp.int32))
    ordering = jnp.argsort(priority, axis=1, stable=True)[:, :B_DEV]
    chosen = (entries[ordering] + favored[column][:, None]) % slab_count
    mixing = jax.vmap(mixed_row)(jax.random.split(jax.random.fold_in(key, 13), device_count))
    chosen = jnp.take_along_axis(chosen, mixing, axis=1).reshape(NORB)
    holder = jnp.repeat(device_ids, B_DEV)
    row_of = jnp.repeat(device_ids // owner_count % row_count, B_DEV)
    inner = jax.random.randint(jax.random.fold_in(key, 14), (NORB,), 0, CZ)
    inner = jnp.where((holder == 0) & (chosen == slab_count - 1), CZ - 1, inner)
    inner = jnp.where((holder == 1) & (chosen == 0), 0, inner)
    plane_pos = chosen * CZ + inner
    row_pos = row_of * CY + jax.random.randint(jax.random.fold_in(key, 15), (NORB,), 0, CY)
    column_pos = jax.random.randint(jax.random.fold_in(key, 16), (NORB,), 0, NX)
    return jnp.stack([plane_pos, row_pos, column_pos], axis=1).astype(jnp.int32)


def shard_levels(stream_key, shape, cuts, low, high):
    level = 1.0
    for axis_at, parts in cuts:
        heights = jax.random.uniform(jax.random.fold_in(jax.random.fold_in(stream_key, 6), axis_at), (parts,), jnp.float32, low / len(cuts), high / len(cuts))
        level = level * jnp.repeat(jnp.exp(heights), shape[axis_at] // parts).reshape((-1,) + (1,) * (len(shape) - 1 - axis_at))
    return level


def gaussian(own_key, extent, spread, most, cuts=(), kind=jnp.bfloat16):
    values = jax.random.normal(own_key, extent, jnp.float32) * spread
    if len(cuts) > 0:
        values = shard_levels(own_key, extent, cuts, -0.22, 0.18) * values
    return jnp.clip(values, min=-most, max=most).astype(kind)


def setup_inputs(seed: int = 0) -> dict:
    seeds = jax.random.split(jax.random.key(seed), 11)
    return {
        "orbitals": gaussian(seeds[0], (NORB, BOX, BOX * BOX), 1.0, 6.0, ((0, 256),)),
        "occupation": jnp.clip(0.5 + 1.5 * jax.random.uniform(seeds[1], (NORB,), jnp.float32) ** shard_levels(seeds[1], (NORB,), ((0, 256),), -0.2, 0.2), 0.5, 2.0),
        "corners": draw_corners(jax.random.fold_in(seeds[10], 71), 0),
        "kernel_widths": jnp.clip(jnp.exp(jax.random.uniform(seeds[3], (CHAN,), jnp.float32, math.log(0.7), math.log(2.5))), 0.7, 2.5),
        "w_in": gaussian(seeds[4], (CHAN, HID), CHAN ** -0.5, 2.0, (), jnp.float32),
        "b_in": gaussian(seeds[5], (HID,), 0.5, 3.0, (), jnp.float32),
        "w_mid": gaussian(seeds[6], (HID, HID), HID ** -0.5, 0.75, (), jnp.float32),
        "b_mid": gaussian(seeds[7], (HID,), 0.5, 3.0, (), jnp.float32),
        "w_out": gaussian(seeds[8], (HID,), HID ** -0.5, 0.75, (), jnp.float32),
        "b_out": gaussian(seeds[9], (1,), 0.5, 3.0, (), jnp.float32),
    }


exact_mode = lax.Precision.HIGHEST


def kernel_taps(kernel_widths):
    offsets = jnp.arange(-RAD, RAD + 1).astype(jnp.float32)
    raw = jnp.exp(-(offsets[None, :] ** 2) / (2.0 * kernel_widths[:, None] ** 2))
    return raw / jnp.sum(raw, axis=1, keepdims=True)


def smooth(padded, weights, planes, rows):
    across = jnp.zeros(padded.shape, jnp.float32)
    for step in range(2 * RAD + 1):
        across = across + weights[step] * jnp.roll(padded, RAD - step, axis=2)
    lines = jnp.zeros((padded.shape[0], rows, padded.shape[2]), jnp.float32)
    for step in range(2 * RAD + 1):
        lines = lines + weights[step] * across[:, step:step + rows]
    result = jnp.zeros((planes, rows, padded.shape[2]), jnp.float32)
    for step in range(2 * RAD + 1):
        result = result + weights[step] * lines[step:step + planes]
    return result


def network(features, w_in, b_in, w_mid, b_mid, w_out, b_out):
    count = features.shape[1]
    blocks = features.reshape(CHAN, count // CELL_BLOCK, CELL_BLOCK).transpose(1, 0, 2)

    def layer_stack(block):
        hidden = jax.nn.silu(jnp.dot(w_in.T, block, precision=exact_mode) + b_in[:, None])
        hidden = jax.nn.silu(jnp.dot(w_mid.T, hidden, precision=exact_mode) + b_mid[:, None])
        return jnp.dot(w_out, hidden, precision=exact_mode) + b_out[0]

    return lax.map(layer_stack, blocks).reshape(count)


def reference(orbitals, occupation, corners, kernel_widths, w_in, b_in, w_mid, b_mid, w_out, b_out):
    orbital_vals = orbitals.astype(jnp.float32)
    box_density = (occupation[:, None, None] * orbital_vals * orbital_vals).astype(jnp.bfloat16)
    anchor = jnp.zeros((), jnp.int32)
    extended = jnp.zeros((NZ + BOX, NY + BOX, NX), jnp.float32)

    def place(index, grid):
        piece = box_density[index].astype(jnp.float32).reshape(BOX, BOX, BOX)
        piece = jnp.pad(piece, ((0, 0), (0, 0), (0, NX - BOX)))
        piece = jnp.roll(piece, corners[index, 2], axis=2)
        start = (corners[index, 0], corners[index, 1], anchor)
        region = lax.dynamic_slice(grid, start, (BOX, BOX, NX))
        return lax.dynamic_update_slice(grid, region + piece, start)

    extended = lax.fori_loop(0, NORB, place, extended)
    folded = extended[:NZ].at[:BOX].add(extended[NZ:])
    density = folded[:, :NY].at[:, :BOX].add(folded[:, NY:])
    taps = kernel_taps(kernel_widths)
    wrapped = jnp.concatenate([density[:, NY - RAD:], density, density[:, :RAD]], axis=1)

    def slab_potential(slab_index):
        plane_ids = (slab_index * CZ - RAD + jnp.arange(CZ + 2 * RAD, dtype=jnp.int32)) % NZ
        padded = jnp.take(wrapped, plane_ids, axis=0)
        features = jnp.stack([jnp.log1p(smooth(padded, taps[channel], CZ, NY)) for channel in range(CHAN)])
        values = network(features.reshape(CHAN, CZ * NY * NX), w_in, b_in, w_mid, b_mid, w_out, b_out)
        return values.reshape(CZ, NY, NX)

    potential = lax.map(slab_potential, jnp.arange(NZ // CZ, dtype=jnp.int32))
    potential = potential.reshape(NZ, NY, NX).astype(jnp.bfloat16)
    wide = jnp.concatenate([potential, potential[:, :BOX]], axis=1)
    reach = jnp.concatenate([wide, wide[:BOX]], axis=0)

    def cut(inputs):
        corner, values = inputs
        window = lax.dynamic_slice(reach, (corner[0], corner[1], anchor), (BOX, BOX, NX))
        window = jnp.roll(window, -corner[2], axis=2)[:, :, :BOX].reshape(BOX, BOX * BOX)
        return (window.astype(jnp.float32) * values).astype(jnp.bfloat16)

    applied = lax.map(cut, (corners, orbital_vals))
    return potential, applied
```

```python
import jax
import jax.numpy as jnp
from jax import lax
from jax.experimental import pallas as pl
from jax.experimental.pallas import tpu as pltpu
from jax.sharding import PartitionSpec as P

BOX = 24
CHAN = 8
HID = 64
RAD = 6
CZ = 24
CY = 24
NX = 128
CAP = 2
SLABS = 16
HELD = 16
HALO = 8
PLANES = CZ + 2 * HALO
HALF = CY // 2
ROWS = HALF + 2 * RAD
REACH = CY + RAD
MAIN = 96
TAIL = CAP * MAIN
BLOCK_ROWS = 224
WINDOW_ROWS = TAIL + BOX

VMEM = pl.BlockSpec(memory_space=pltpu.VMEM)
SMEM = pl.BlockSpec(memory_space=pltpu.SMEM)
f32 = jnp.float32
bf16 = jnp.bfloat16


def shifted(x, axis, by):
    count = lax.axis_size(axis)
    return lax.ppermute(x, axis, [(i, (i + by) % count) for i in range(count)])


def from_next_other(x):
    tiles, owners = lax.axis_size("gy"), lax.axis_size("orb")
    pairs = [
        ((tile + 1) % tiles * owners + (orb + 1) % owners, tile * owners + orb)
        for tile in range(tiles)
        for orb in range(owners)
    ]
    return lax.ppermute(x, ("gy", "orb"), pairs)


def split(x):
    high = x.astype(bf16)
    return high, (x - high.astype(f32)).astype(bf16)


def split_table(x):
    high = lax.reduce_precision(x, 8, 7)
    return high.astype(bf16), (x - high).astype(bf16)


def lanes(rows):
    return lax.broadcasted_iota(jnp.int32, (rows, NX), 1)


def pack_body(corners, occupation, orbitals, sent, count):
    sent[...] = jnp.zeros(sent.shape, bf16)

    def clear(slab, carry):
        count[slab] = 0
        return carry

    lax.fori_loop(0, SLABS, clear, 0)
    side = lanes(32) // 64
    field = lanes(8) % 64

    def place(i, carry):
        plane = corners[i, 0]
        row = corners[i, 1]
        column = corners[i, 2]
        slab = lax.div(plane, CZ)
        rank = count[slab]
        count[slab] = rank + 1
        values = orbitals[i].astype(f32)
        density = occupation[i] * values * values
        main = jnp.concatenate([density[:, 128 * j : 128 * j + 128] for j in range(4)], axis=0)
        sent[slab, pl.ds(pl.multiple_of(rank * MAIN, 32), MAIN), :] = main.astype(bf16)
        last = density[:, 512:576]
        tail = jnp.concatenate([last, last], axis=1)
        offsets = jnp.where(
            field == 0,
            lax.rem(plane, CZ),
            jnp.where(field == 1, lax.rem(row, CY), jnp.where(field == 2, column, 0)),
        ).astype(f32)
        fresh = jnp.concatenate([tail, offsets], axis=0)
        held = sent[slab, TAIL:BLOCK_ROWS, :].astype(f32)
        sent[slab, TAIL:BLOCK_ROWS, :] = jnp.where(side == rank, fresh, held).astype(bf16)
        return carry

    lax.fori_loop(0, HELD, place, 0)


def pack(corners, occupation, orbitals):
    return pl.pallas_call(
        pack_body,
        name="pack_boxes",
        out_shape=jax.ShapeDtypeStruct((SLABS, BLOCK_ROWS, NX), bf16),
        in_specs=[SMEM, SMEM, VMEM],
        out_specs=VMEM,
        scratch_shapes=[pltpu.SMEM((SLABS,), jnp.int32)],
    )(corners, occupation, orbitals)


def read_offsets(received, rows, offsets, sem):
    for source in range(SLABS):
        rows[source : source + 1, :] = (
            received[source, 208:BLOCK_ROWS, :].astype(f32)[8:9].astype(jnp.int32)
        )
    copy = pltpu.make_async_copy(rows, offsets, sem)
    copy.start()
    return copy


def deposit_body(received, own, next_up, second_up, next_down, offsets_out, grid, rows, offsets, sem):
    copy = read_offsets(received, rows, offsets, sem)
    offsets_out[...] = rows[...]
    grid[...] = jnp.zeros(grid.shape, f32)
    copy.wait()
    lane = lanes(BOX)

    def source_step(source, carry):
        tail_both = received[source, TAIL:BLOCK_ROWS, :].astype(f32)[:BOX]
        for slot in range(CAP):
            z0 = offsets[source, 64 * slot]
            y0 = offsets[source, 64 * slot + 1]
            x0 = offsets[source, 64 * slot + 2]
            main = received[source, MAIN * slot : MAIN * slot + MAIN, :].astype(f32)
            tiles = [main[BOX * j : BOX * j + BOX] for j in range(4)]
            tiles.append(tail_both if slot == 0 else pltpu.roll(tail_both, 64, 1))
            inside = ((lane - x0) & (NX - 1)) < BOX
            for first in range(0, BOX, 8):
                olds = [
                    grid[y0 + b, pl.ds(z0, BOX), :] for b in range(first, first + 8)
                ]
                news = []
                for k in range(8):
                    b = first + k
                    tile, left = divmod(BOX * b, NX)
                    piece = tiles[tile]
                    if left + BOX > NX:
                        piece = jnp.where(lane >= left, piece, tiles[tile + 1])
                    piece = pltpu.roll(piece, (x0 - left) & (NX - 1), 1)
                    news.append(olds[k] + jnp.where(inside, piece, 0.0))
                for k in range(8):
                    grid[y0 + first + k, pl.ds(z0, BOX), :] = news[k]
        return carry

    lax.fori_loop(0, SLABS, source_step, 0)
    own[...] = grid[:, : PLANES - HALO, :]
    next_up[...] = grid[:, CZ - HALO :, :].astype(bf16)
    second_up[...] = grid[:, 2 * CZ - HALO :, :].astype(bf16)
    next_down[...] = grid[:, :HALO, :].astype(bf16)


def deposit(received):
    return pl.pallas_call(
        deposit_body,
        name="deposit_boxes",
        out_shape=(
            jax.ShapeDtypeStruct((CY + BOX, PLANES - HALO, NX), f32),
            jax.ShapeDtypeStruct((CY + BOX, PLANES - HALO, NX), bf16),
            jax.ShapeDtypeStruct((CY + BOX, HALO, NX), bf16),
            jax.ShapeDtypeStruct((CY + BOX, HALO, NX), bf16),
            jax.ShapeDtypeStruct((SLABS, NX), jnp.int32),
        ),
        in_specs=[VMEM],
        out_specs=(VMEM,) * 5,
        scratch_shapes=[
            pltpu.VMEM((CY + BOX, CZ + BOX, NX), f32),
            pltpu.VMEM((SLABS, NX), jnp.int32),
            pltpu.SMEM((SLABS, NX), jnp.int32),
            pltpu.SemaphoreType.DMA,
        ],
    )(received)


def fold_planes_body(own, below, second_below, above, kept, next_right, second_right, next_left):
    for first, last in ((0, HALO), (HALO, PLANES - HALO), (PLANES - HALO, PLANES)):
        total = None
        parts = []
        if last > HALO:
            parts.append(own[:, first - HALO : last - HALO, :])
        if last <= PLANES - HALO:
            parts.append(below[:, first:last, :].astype(f32))
        if last == HALO:
            parts.append(second_below[...].astype(f32))
        if first == PLANES - HALO:
            parts.append(above[...].astype(f32))
        total = parts[0]
        for part in parts[1:]:
            total = total + part
        kept[:, first:last, :] = total[:REACH]
        next_right[:, first:last, :] = total[CY - RAD :].astype(bf16)
        second_right[:, first:last, :] = total[2 * CY - RAD :].astype(bf16)
        next_left[:, first:last, :] = total[:RAD].astype(bf16)


def fold_planes(own, below, second_below, above):
    return pl.pallas_call(
        fold_planes_body,
        name="fold_planes",
        out_shape=(
            jax.ShapeDtypeStruct((REACH, PLANES, NX), f32),
            jax.ShapeDtypeStruct((REACH, PLANES, NX), bf16),
            jax.ShapeDtypeStruct((RAD, PLANES, NX), bf16),
            jax.ShapeDtypeStruct((RAD, PLANES, NX), bf16),
        ),
        in_specs=[VMEM] * 4,
        out_specs=(VMEM,) * 4,
    )(own, below, second_below, above)


def fold_rows_body(position, own, left, second_left, right, kept, given, total):
    for first, last in ((0, RAD), (RAD, REACH), (REACH, REACH + RAD)):
        parts = []
        if last > RAD:
            parts.append(own[first - RAD : last - RAD])
        if last <= REACH:
            parts.append(left[first:last].astype(f32))
        if last == RAD:
            parts.append(second_left[...].astype(f32))
        if first == REACH:
            parts.append(right[...].astype(f32))
        row_total = parts[0]
        for part in parts[1:]:
            row_total = row_total + part
        total[first:last] = row_total
    orb = position[0]
    kept[...] = total[pl.ds(HALF * orb, ROWS)]
    given[...] = total[pl.ds(HALF * (1 - orb), ROWS)].astype(bf16)


def fold_rows(position, own, left, second_left, right):
    return pl.pallas_call(
        fold_rows_body,
        name="fold_rows",
        out_shape=(
            jax.ShapeDtypeStruct((ROWS, PLANES, NX), f32),
            jax.ShapeDtypeStruct((ROWS, PLANES, NX), bf16),
        ),
        in_specs=[SMEM] + [VMEM] * 4,
        out_specs=(VMEM, VMEM),
        scratch_shapes=[pltpu.VMEM((REACH + RAD, PLANES, NX), f32)],
    )(position, own, left, second_left, right)


def model_body(
    taps,
    kept,
    other,
    plane_table,
    column_table,
    first_table,
    middle_table,
    middle_bias,
    last_weight,
    last_bias,
    potential,
    planes,
    features,
    result,
):
    def plane_step(pair, carry):
        density = kept[pl.ds(2 * pair, 2)] + other[pl.ds(2 * pair, 2)].astype(f32)
        density = density.astype(bf16)
        field = jnp.concatenate([density[0], density[1]], axis=1)
        both = jnp.dot(plane_table[...], field, preferred_element_type=f32)
        total = both[: CHAN * CZ] + both[CHAN * CZ :]
        planes[2 * pair] = total[:, :NX]
        planes[2 * pair + 1] = total[:, NX:]
        return carry

    lax.fori_loop(0, ROWS // 2, plane_step, 0, unroll=2)

    def channel_step(channel, carry):
        weights = [taps[channel, step] for step in range(RAD + 1)]
        lines = []
        for part in range(CZ // 8):
            start = pl.multiple_of(channel * CZ + 8 * part, 8)
            rows = [planes[y, pl.ds(start, 8), :] for y in range(ROWS)]
            for y in range(HALF):
                total = weights[RAD] * rows[y + RAD]
                for step in range(RAD):
                    total = total + weights[step] * (rows[y + step] + rows[y + 2 * RAD - step])
                lines.append(total)
        high, low = split(jnp.concatenate(lines, axis=0))
        both = jnp.dot(
            jnp.concatenate([high, low], axis=1), column_table[channel], preferred_element_type=f32
        )
        smooth = both[:, :NX] + both[:, NX:]
        features[channel] = jnp.log(1.0 + smooth)
        return carry

    lax.fori_loop(0, CHAN, channel_step, 0)

    def cell_step(step, carry):
        start = pl.multiple_of(step * 16, 16)
        inputs = [features[channel, pl.ds(start, 16), :] for channel in range(CHAN)]
        cells = jnp.concatenate(
            [
                jnp.concatenate([piece[:8] for piece in inputs], axis=0),
                jnp.concatenate([piece[8:] for piece in inputs], axis=0),
            ],
            axis=1,
        )
        high, low = split(cells)
        ones = jnp.ones((16, 2 * NX), bf16)
        stacked = jnp.concatenate([high, low, high, ones], axis=0)
        values = []
        for half in range(2):
            hidden = jnp.dot(
                first_table[256 * half : 256 * half + 256, :], stacked, preferred_element_type=f32
            )
            hidden = hidden + hidden * jnp.tanh(hidden)
            hidden_high, hidden_low = split(hidden)
            for pair in range(2):
                rows = slice(128 * pair, 128 * pair + 128)
                both = jnp.dot(
                    middle_table[...],
                    jnp.concatenate([hidden_high[rows], hidden_low[rows]], axis=0),
                    preferred_element_type=f32,
                )
                mixed = both[:128] + both[128:] + middle_bias[...]
                mixed = (mixed + mixed * jnp.tanh(mixed)) * last_weight[...]
                values.append(jnp.sum(mixed.reshape(2, HID, 2 * NX), axis=1))
        value = jnp.concatenate(values, axis=0) + last_bias[0]
        result[pl.ds(start, 8), :] = value[:, :NX]
        result[pl.ds(start + 8, 8), :] = value[:, NX:]
        return carry

    lax.fori_loop(0, CZ * HALF // 16, cell_step, 0, unroll=3)
    for part in range(CZ // 8):
        block = result[HALF * 8 * part : HALF * 8 * (part + 1), :]
        planes[:HALF, 8 * part : 8 * part + 8, :] = block.reshape(HALF, 8, NX)
    potential[...] = planes[:HALF, :CZ, :].astype(bf16)


def model(kept, other, taps, tables):
    return pl.pallas_call(
        model_body,
        name="smooth_and_network",
        out_shape=jax.ShapeDtypeStruct((HALF, CZ, NX), bf16),
        in_specs=[SMEM] + [VMEM] * 8 + [SMEM],
        out_specs=VMEM,
        scratch_shapes=[
            pltpu.VMEM((ROWS, CHAN * CZ, NX), f32),
            pltpu.VMEM((CHAN, HALF * CZ, NX), f32),
            pltpu.VMEM((HALF * CZ, NX), f32),
        ],
        compiler_params=pltpu.CompilerParams(vmem_limit_bytes=48 * 1024 * 1024),
    )(taps, kept, other, *tables)


def kernel_taps(kernel_widths):
    offsets = jnp.arange(-RAD, RAD + 1).astype(f32)
    raw = jnp.exp(-(offsets[None, :] ** 2) / (2.0 * kernel_widths[:, None] ** 2))
    return raw / jnp.sum(raw, axis=1, keepdims=True)


def tap_table(taps, distance):
    table = jnp.zeros((taps.shape[0],) + distance.shape, f32)
    for step in range(2 * RAD + 1):
        table = table + taps[:, step][:, None, None] * (distance == step).astype(f32)[None]
    return table


def model_tables(taps, w_in, b_in, w_mid, b_mid, w_out, b_out):
    out_index = jnp.arange(CZ, dtype=jnp.int32)
    in_index = jnp.arange(PLANES, dtype=jnp.int32) - (HALO - RAD)
    plane = tap_table(taps, in_index[None, :] - out_index[:, None]).reshape(CHAN * CZ, PLANES)
    plane_table = jnp.concatenate(split_table(plane), axis=0)
    source = jnp.arange(NX, dtype=jnp.int32)
    column = tap_table(taps, (source[:, None] - source[None, :] + RAD) % NX)
    column_high, column_low = split_table(column)
    column_table = jnp.concatenate(
        [
            jnp.concatenate([column_high, column_low], axis=2),
            jnp.concatenate([column_high, jnp.zeros_like(column_low)], axis=2),
        ],
        axis=1,
    )
    eight = jnp.eye(8, dtype=f32)
    first = (0.5 * w_in.T)[None, :, :, None] * eight[:, None, None, :]
    first_high, first_low = split_table(first.reshape(8 * HID, CHAN * 8))
    bias_high, bias_low = split_table(jnp.tile(0.5 * b_in, 8)[:, None])
    first_table = jnp.concatenate(
        [
            first_high,
            first_high,
            first_low,
            bias_high,
            bias_low,
            jnp.zeros((8 * HID, 14), bf16),
        ],
        axis=1,
    )
    two = jnp.eye(2, dtype=f32)
    middle = (two[:, None, :, None] * (0.5 * w_mid.T)[None, :, None, :]).reshape(2 * HID, 2 * HID)
    middle_high, middle_low = split_table(middle)
    middle_table = jnp.concatenate(
        [
            jnp.concatenate([middle_high, middle_high], axis=1),
            jnp.concatenate([middle_low, jnp.zeros_like(middle_low)], axis=1),
        ],
        axis=0,
    )
    middle_bias = jnp.broadcast_to(jnp.tile(0.5 * b_mid, 2)[:, None], (2 * HID, 2 * NX))
    last_weight = jnp.broadcast_to(jnp.tile(w_out, 2)[:, None], (2 * HID, 2 * NX))
    return (
        plane_table,
        column_table,
        first_table,
        middle_table,
        middle_bias,
        last_weight,
        b_out,
    )


def widen_body(position, own, partner, next_same, next_other, wide):
    orb = position[0]
    wide[pl.ds(HALF * orb, HALF)] = own[...]
    wide[pl.ds(HALF * (1 - orb), HALF)] = partner[...]
    wide[pl.ds(CY + HALF * orb, HALF)] = next_same[...]
    wide[pl.ds(CY + HALF * (1 - orb), HALF)] = next_other[...]


def widen(position, own, partner, next_same, next_other):
    return pl.pallas_call(
        widen_body,
        name="widen_rows",
        out_shape=jax.ShapeDtypeStruct((CY + BOX, CZ, NX), bf16),
        in_specs=[SMEM] + [VMEM] * 4,
        out_specs=VMEM,
    )(position, own, partner, next_same, next_other)


def cut_body(offsets, wide, beyond, windows, reach):
    reach[:, :CZ, :] = wide[...].astype(f32)
    reach[:, CZ:, :] = beyond[...].astype(f32)
    lane = lanes(BOX)

    def source_step(source, carry):
        mains, tails = [], []
        for slot in range(CAP):
            z0 = offsets[source, 64 * slot]
            y0 = offsets[source, 64 * slot + 1]
            x0 = offsets[source, 64 * slot + 2]
            tiles = [None] * 5
            for b in range(BOX):
                tile, left = divmod(BOX * b, NX)
                piece = reach[y0 + b, pl.ds(z0, BOX), :]
                piece = pltpu.roll(piece, (left - x0) & (NX - 1), 1)
                if tiles[tile] is None:
                    tiles[tile] = piece
                else:
                    tiles[tile] = jnp.where(lane >= left, piece, tiles[tile])
                if left + BOX > NX:
                    tiles[tile + 1] = piece
            mains += tiles[:4]
            tails.append(tiles[4])
        tail = jnp.where(lane < 64, tails[0], pltpu.roll(tails[1], 64, 1))
        windows[source] = jnp.concatenate(mains + [tail], axis=0).astype(bf16)
        return carry

    lax.fori_loop(0, SLABS, source_step, 0)


def cut(offsets, wide, beyond):
    return pl.pallas_call(
        cut_body,
        name="cut_windows",
        out_shape=jax.ShapeDtypeStruct((SLABS, WINDOW_ROWS, NX), bf16),
        in_specs=[SMEM, VMEM, VMEM],
        out_specs=VMEM,
        scratch_shapes=[pltpu.VMEM((CY + BOX, CZ + BOX, NX), f32)],
    )(offsets, wide, beyond)


def apply_body(corners, windows, orbitals, applied, count):
    def clear(slab, carry):
        count[slab] = 0
        return carry

    lax.fori_loop(0, SLABS, clear, 0)

    def place(i, carry):
        slab = lax.div(corners[i, 0], CZ)
        rank = count[slab]
        count[slab] = rank + 1
        main = windows[slab, pl.ds(pl.multiple_of(rank * MAIN, 32), MAIN), :].astype(f32)
        tail = windows[slab, TAIL:WINDOW_ROWS, :].astype(f32)
        tail = jnp.where(rank == 0, tail[:, :64], tail[:, 64:])
        whole = jnp.concatenate([main[BOX * j : BOX * j + BOX] for j in range(4)] + [tail], axis=1)
        applied[i] = (whole * orbitals[i].astype(f32)).astype(bf16)
        return carry

    lax.fori_loop(0, HELD, place, 0)


def apply(corners, windows, orbitals):
    return pl.pallas_call(
        apply_body,
        name="apply_windows",
        out_shape=jax.ShapeDtypeStruct(orbitals.shape, bf16),
        in_specs=[SMEM, VMEM, VMEM],
        out_specs=VMEM,
        scratch_shapes=[pltpu.SMEM((SLABS,), jnp.int32)],
    )(corners, windows, orbitals)


def exchange(x, axis):
    return lax.all_to_all(x, axis, split_axis=0, concat_axis=0, tiled=True)


def local(orbitals, occupation, corners, kernel_widths, w_in, b_in, w_mid, b_mid, w_out, b_out):
    taps = kernel_taps(kernel_widths)
    tables = model_tables(taps, w_in, b_in, w_mid, b_mid, w_out, b_out)
    received = exchange(pack(corners, occupation, orbitals), "gz")
    position = lax.axis_index("orb").reshape(1)
    own, next_up, second_up, next_down, offsets = deposit(received)
    below = shifted(next_up, "gz", 1)
    second_below = shifted(second_up, "gz", 2)
    above = shifted(next_down, "gz", -1)
    kept, next_right, second_right, next_left = fold_planes(own, below, second_below, above)
    left = shifted(next_right, "gy", 1)
    second_left = shifted(second_right, "gy", 2)
    right = shifted(next_left, "gy", -1)
    kept, given = fold_rows(position, kept, left, second_left, right)
    half = model(kept, shifted(given, "orb", 1), taps, tables)
    partner = shifted(half, "orb", 1)
    next_same = shifted(half, "gy", -1)
    next_other = from_next_other(half)
    wide = widen(position, half, partner, next_same, next_other)
    windows = cut(offsets, wide, shifted(wide, "gz", -1))
    applied = apply(corners, exchange(windows, "gz"), orbitals)
    return jnp.transpose(wide[:CY], (1, 0, 2)), applied


def solution(mesh):
    return jax.shard_map(
        local,
        mesh=mesh,
        in_specs=(
            P(("gz", "gy", "orb"), None, None),
            P(("gz", "gy", "orb")),
            P(("gz", "gy", "orb"), None),
            P(),
            P(),
            P(),
            P(),
            P(),
            P(),
            P(),
        ),
        out_specs=(P("gz", "gy", None), P(("gz", "gy", "orb"), None, None)),
        check_vma=False,
    )
```

```python
import jax
import jax.numpy as jnp
from jax import lax
from jax.experimental import pallas as pl
from jax.experimental.pallas import tpu as pltpu
from jax.sharding import PartitionSpec as P

BOX = 24
CHAN = 8
HID = 64
RAD = 6
CZ = 24
CY = 24
NX = 128
CAP = 2
SLABS = 16
HELD = 16
HALO = 8
PLANES = CZ + 2 * HALO
HALF = CY // 2
ROWS = HALF + 2 * RAD
REACH = CY + RAD
MAIN = 96
TAIL = CAP * MAIN
BLOCK_ROWS = 224
WINDOW_ROWS = TAIL + BOX

VMEM = pl.BlockSpec(memory_space=pltpu.VMEM)
SMEM = pl.BlockSpec(memory_space=pltpu.SMEM)
ROOM = pltpu.CompilerParams(vmem_limit_bytes=16 * 1024 * 1024)
f32 = jnp.float32
bf16 = jnp.bfloat16


def shifted(x, axis, by):
    count = lax.axis_size(axis)
    return lax.ppermute(x, axis, [(i, (i + by) % count) for i in range(count)])


def crossed(x, by):
    tiles, owners = lax.axis_size("gy"), lax.axis_size("orb")
    pairs = [
        (tile * owners + orb, (tile + by) % tiles * owners + (orb + 1) % owners)
        for tile in range(tiles)
        for orb in range(owners)
    ]
    return lax.ppermute(x, ("gy", "orb"), pairs)


def split(x):
    high = x.astype(bf16)
    return high, (x - high.astype(f32)).astype(bf16)


def split_table(x):
    high = lax.reduce_precision(x, 8, 7)
    return high.astype(bf16), (x - high).astype(bf16)


def lanes(rows):
    return lax.broadcasted_iota(jnp.int32, (rows, NX), 1)


def pack_body(corners, occupation, orbitals, sent, count):
    sent[...] = jnp.zeros(sent.shape, bf16)

    def clear(slab, carry):
        count[slab] = 0
        return carry

    lax.fori_loop(0, SLABS, clear, 0)
    side = lanes(32) // 64
    field = lanes(8) % 64

    def place(i, carry):
        plane = corners[0, i]
        row = corners[1, i]
        column = corners[2, i]
        slab = lax.div(plane, CZ)
        rank = count[slab]
        count[slab] = rank + 1
        values = orbitals[i].astype(f32)
        density = occupation[i] * values * values
        main = jnp.concatenate([density[:, 128 * j : 128 * j + 128] for j in range(4)], axis=0)
        sent[slab, pl.ds(pl.multiple_of(rank * MAIN, 32), MAIN), :] = main.astype(bf16)
        last = density[:, 512:576]
        tail = jnp.concatenate([last, last], axis=1)
        offsets = jnp.where(
            field == 0,
            lax.rem(plane, CZ),
            jnp.where(field == 1, lax.rem(row, CY), jnp.where(field == 2, column, 0)),
        ).astype(f32)
        fresh = jnp.concatenate([tail, offsets], axis=0)
        held = sent[slab, TAIL:BLOCK_ROWS, :].astype(f32)
        sent[slab, TAIL:BLOCK_ROWS, :] = jnp.where(side == rank, fresh, held).astype(bf16)
        return carry

    lax.fori_loop(0, HELD, place, 0)


def pack(corners, occupation, orbitals):
    return pl.pallas_call(
        pack_body,
        name="pack_boxes",
        out_shape=jax.ShapeDtypeStruct((SLABS, BLOCK_ROWS, NX), bf16),
        in_specs=[SMEM, SMEM, VMEM],
        out_specs=VMEM,
        scratch_shapes=[pltpu.SMEM((SLABS,), jnp.int32)],
        compiler_params=ROOM,
    )(corners, occupation, orbitals)


def read_offsets(received, rows, offsets, sem):
    for source in range(SLABS):
        rows[source : source + 1, :] = (
            received[source, 208:BLOCK_ROWS, :].astype(f32)[8:9].astype(jnp.int32)
        )
    copy = pltpu.make_async_copy(rows, offsets, sem)
    copy.start()
    return copy


def deposit_body(received, own, next_up, second_up, next_down, offsets_out, grid, rows, offsets, sem):
    copy = read_offsets(received, rows, offsets, sem)
    offsets_out[...] = rows[...]
    grid[...] = jnp.zeros(grid.shape, f32)
    copy.wait()
    lane = lanes(BOX)

    def source_step(source, carry):
        tail_both = received[source, TAIL:BLOCK_ROWS, :].astype(f32)[:BOX]
        for slot in range(CAP):
            z0 = offsets[source, 64 * slot]
            y0 = offsets[source, 64 * slot + 1]
            x0 = offsets[source, 64 * slot + 2]
            main = received[source, MAIN * slot : MAIN * slot + MAIN, :].astype(f32)
            tiles = [main[BOX * j : BOX * j + BOX] for j in range(4)]
            tiles.append(tail_both if slot == 0 else pltpu.roll(tail_both, 64, 1))
            inside = ((lane - x0) & (NX - 1)) < BOX
            for first in range(0, BOX, 8):
                olds = [
                    grid[y0 + b, pl.ds(z0, BOX), :] for b in range(first, first + 8)
                ]
                news = []
                for k in range(8):
                    b = first + k
                    tile, left = divmod(BOX * b, NX)
                    piece = tiles[tile]
                    if left + BOX > NX:
                        piece = jnp.where(lane >= left, piece, tiles[tile + 1])
                    piece = pltpu.roll(piece, (x0 - left) & (NX - 1), 1)
                    news.append(olds[k] + jnp.where(inside, piece, 0.0))
                for k in range(8):
                    grid[y0 + first + k, pl.ds(z0, BOX), :] = news[k]
        return carry

    lax.fori_loop(0, SLABS, source_step, 0)
    own[...] = grid[:, : PLANES - HALO, :]
    next_up[...] = grid[:, CZ - HALO :, :].astype(bf16)
    second_up[...] = grid[:, 2 * CZ - HALO :, :].astype(bf16)
    next_down[...] = grid[:, :HALO, :].astype(bf16)


def deposit(received):
    return pl.pallas_call(
        deposit_body,
        name="deposit_boxes",
        out_shape=(
            jax.ShapeDtypeStruct((CY + BOX, PLANES - HALO, NX), f32),
            jax.ShapeDtypeStruct((CY + BOX, PLANES - HALO, NX), bf16),
            jax.ShapeDtypeStruct((CY + BOX, HALO, NX), bf16),
            jax.ShapeDtypeStruct((CY + BOX, HALO, NX), bf16),
            jax.ShapeDtypeStruct((SLABS, NX), jnp.int32),
        ),
        in_specs=[VMEM],
        out_specs=(VMEM,) * 5,
        scratch_shapes=[
            pltpu.VMEM((CY + BOX, CZ + BOX, NX), f32),
            pltpu.VMEM((SLABS, NX), jnp.int32),
            pltpu.SMEM((SLABS, NX), jnp.int32),
            pltpu.SemaphoreType.DMA,
        ],
        compiler_params=ROOM,
    )(received)


def fold_planes_body(own, below, second_below, above, kept, next_right, second_right, next_left):
    for first, last in ((0, HALO), (HALO, PLANES - HALO), (PLANES - HALO, PLANES)):
        total = None
        parts = []
        if last > HALO:
            parts.append(own[:, first - HALO : last - HALO, :])
        if last <= PLANES - HALO:
            parts.append(below[:, first:last, :].astype(f32))
        if last == HALO:
            parts.append(second_below[...].astype(f32))
        if first == PLANES - HALO:
            parts.append(above[...].astype(f32))
        total = parts[0]
        for part in parts[1:]:
            total = total + part
        kept[:, first:last, :] = total[:REACH]
        next_right[:, first:last, :] = total[CY - RAD :].astype(bf16)
        second_right[:, first:last, :] = total[2 * CY - RAD :].astype(bf16)
        next_left[:, first:last, :] = total[:RAD].astype(bf16)


def fold_planes(own, below, second_below, above):
    return pl.pallas_call(
        fold_planes_body,
        name="fold_planes",
        out_shape=(
            jax.ShapeDtypeStruct((REACH, PLANES, NX), f32),
            jax.ShapeDtypeStruct((REACH, PLANES, NX), bf16),
            jax.ShapeDtypeStruct((RAD, PLANES, NX), bf16),
            jax.ShapeDtypeStruct((RAD, PLANES, NX), bf16),
        ),
        in_specs=[VMEM] * 4,
        out_specs=(VMEM,) * 4,
        compiler_params=ROOM,
    )(own, below, second_below, above)


def fold_rows_body(position, own, left, second_left, right, kept, given, total):
    for first, last in ((0, RAD), (RAD, REACH), (REACH, REACH + RAD)):
        parts = []
        if last > RAD:
            parts.append(own[first - RAD : last - RAD])
        if last <= REACH:
            parts.append(left[first:last].astype(f32))
        if last == RAD:
            parts.append(second_left[...].astype(f32))
        if first == REACH:
            parts.append(right[...].astype(f32))
        row_total = parts[0]
        for part in parts[1:]:
            row_total = row_total + part
        total[first:last] = row_total
    orb = position[0]
    kept[...] = total[pl.ds(HALF * orb, ROWS)]
    given[...] = total[pl.ds(HALF * (1 - orb), ROWS)].astype(bf16)


def fold_rows(position, own, left, second_left, right):
    return pl.pallas_call(
        fold_rows_body,
        name="fold_rows",
        out_shape=(
            jax.ShapeDtypeStruct((ROWS, PLANES, NX), f32),
            jax.ShapeDtypeStruct((ROWS, PLANES, NX), bf16),
        ),
        in_specs=[SMEM] + [VMEM] * 4,
        out_specs=(VMEM, VMEM),
        scratch_shapes=[pltpu.VMEM((REACH + RAD, PLANES, NX), f32)],
        compiler_params=ROOM,
    )(position, own, left, second_left, right)


def model_body(
    taps,
    kept,
    other,
    plane_table,
    column_table,
    first_table,
    middle_table,
    middle_bias,
    last_weight,
    last_bias,
    potential,
    planes,
    features,
    result,
):
    def plane_step(pair, carry):
        density = kept[pl.ds(2 * pair, 2)] + other[pl.ds(2 * pair, 2)].astype(f32)
        density = density.astype(bf16)
        field = jnp.concatenate([density[0], density[1]], axis=1)
        both = jnp.dot(plane_table[...], field, preferred_element_type=f32)
        total = both[: CHAN * CZ] + both[CHAN * CZ :]
        planes[2 * pair] = total[:, :NX]
        planes[2 * pair + 1] = total[:, NX:]
        return carry

    lax.fori_loop(0, ROWS // 2, plane_step, 0, unroll=2)

    def channel_step(channel, carry):
        weights = [taps[channel, step] for step in range(RAD + 1)]
        lines = []
        for part in range(CZ // 8):
            start = pl.multiple_of(channel * CZ + 8 * part, 8)
            rows = [planes[y, pl.ds(start, 8), :] for y in range(ROWS)]
            for y in range(HALF):
                total = weights[RAD] * rows[y + RAD]
                for step in range(RAD):
                    total = total + weights[step] * (rows[y + step] + rows[y + 2 * RAD - step])
                lines.append(total)
        high, low = split(jnp.concatenate(lines, axis=0))
        both = jnp.dot(
            jnp.concatenate([high, low], axis=1), column_table[channel], preferred_element_type=f32
        )
        smooth = both[:, :NX] + both[:, NX:]
        features[channel] = jnp.log(1.0 + smooth)
        return carry

    lax.fori_loop(0, CHAN, channel_step, 0)

    def cell_step(step, carry):
        start = pl.multiple_of(step * 16, 16)
        inputs = [features[channel, pl.ds(start, 16), :] for channel in range(CHAN)]
        cells = jnp.concatenate(
            [
                jnp.concatenate([piece[:8] for piece in inputs], axis=0),
                jnp.concatenate([piece[8:] for piece in inputs], axis=0),
            ],
            axis=1,
        )
        high, low = split(cells)
        ones = jnp.ones((16, 2 * NX), bf16)
        stacked = jnp.concatenate([high, low, high, ones], axis=0)
        values = []
        for half in range(2):
            hidden = jnp.dot(
                first_table[256 * half : 256 * half + 256, :], stacked, preferred_element_type=f32
            )
            hidden = hidden + hidden * jnp.tanh(hidden)
            hidden_high, hidden_low = split(hidden)
            for pair in range(2):
                rows = slice(128 * pair, 128 * pair + 128)
                both = jnp.dot(
                    middle_table[...],
                    jnp.concatenate([hidden_high[rows], hidden_low[rows]], axis=0),
                    preferred_element_type=f32,
                )
                mixed = both[:128] + both[128:] + middle_bias[...]
                mixed = (mixed + mixed * jnp.tanh(mixed)) * last_weight[...]
                values.append(jnp.sum(mixed.reshape(2, HID, 2 * NX), axis=1))
        value = jnp.concatenate(values, axis=0) + last_bias[0]
        result[pl.ds(start, 8), :] = value[:, :NX]
        result[pl.ds(start + 8, 8), :] = value[:, NX:]
        return carry

    lax.fori_loop(0, CZ * HALF // 16, cell_step, 0, unroll=3)
    for part in range(CZ // 8):
        block = result[HALF * 8 * part : HALF * 8 * (part + 1), :]
        planes[:HALF, 8 * part : 8 * part + 8, :] = block.reshape(HALF, 8, NX)
    potential[...] = planes[:HALF, :CZ, :].astype(bf16)


def model(kept, other, taps, tables):
    return pl.pallas_call(
        model_body,
        name="smooth_and_network",
        out_shape=jax.ShapeDtypeStruct((HALF, CZ, NX), bf16),
        in_specs=[SMEM] + [VMEM] * 8 + [SMEM],
        out_specs=VMEM,
        scratch_shapes=[
            pltpu.VMEM((ROWS, CHAN * CZ, NX), f32),
            pltpu.VMEM((CHAN, HALF * CZ, NX), f32),
            pltpu.VMEM((HALF * CZ, NX), f32),
        ],
        compiler_params=ROOM,
    )(taps, kept, other, *tables)


def kernel_taps(kernel_widths):
    offsets = jnp.arange(-RAD, RAD + 1).astype(f32)
    raw = jnp.exp(-(offsets[None, :] ** 2) / (2.0 * kernel_widths[:, None] ** 2))
    return raw / jnp.sum(raw, axis=1, keepdims=True)


def tap_table(taps, distance):
    table = jnp.zeros((taps.shape[0],) + distance.shape, f32)
    for step in range(2 * RAD + 1):
        table = table + taps[:, step][:, None, None] * (distance == step).astype(f32)[None]
    return table


def model_tables(taps, w_in, b_in, w_mid, b_mid, w_out, b_out):
    out_index = jnp.arange(CZ, dtype=jnp.int32)
    in_index = jnp.arange(PLANES, dtype=jnp.int32) - (HALO - RAD)
    plane = tap_table(taps, in_index[None, :] - out_index[:, None]).reshape(CHAN * CZ, PLANES)
    plane_table = jnp.concatenate(split_table(plane), axis=0)
    source = jnp.arange(NX, dtype=jnp.int32)
    column = tap_table(taps, (source[:, None] - source[None, :] + RAD) % NX)
    column_high, column_low = split_table(column)
    column_table = jnp.concatenate(
        [
            jnp.concatenate([column_high, column_low], axis=2),
            jnp.concatenate([column_high, jnp.zeros_like(column_low)], axis=2),
        ],
        axis=1,
    )
    eight = jnp.eye(8, dtype=f32)
    first = (0.5 * w_in.T)[None, :, :, None] * eight[:, None, None, :]
    first_high, first_low = split_table(first.reshape(8 * HID, CHAN * 8))
    bias_high, bias_low = split_table(jnp.tile(0.5 * b_in, 8)[:, None])
    first_table = jnp.concatenate(
        [
            first_high,
            first_high,
            first_low,
            bias_high,
            bias_low,
            jnp.zeros((8 * HID, 14), bf16),
        ],
        axis=1,
    )
    two = jnp.eye(2, dtype=f32)
    middle = (two[:, None, :, None] * (0.5 * w_mid.T)[None, :, None, :]).reshape(2 * HID, 2 * HID)
    middle_high, middle_low = split_table(middle)
    middle_table = jnp.concatenate(
        [
            jnp.concatenate([middle_high, middle_high], axis=1),
            jnp.concatenate([middle_low, jnp.zeros_like(middle_low)], axis=1),
        ],
        axis=0,
    )
    middle_bias = jnp.broadcast_to(jnp.tile(0.5 * b_mid, 2)[:, None], (2 * HID, 2 * NX))
    last_weight = jnp.broadcast_to(jnp.tile(w_out, 2)[:, None], (2 * HID, 2 * NX))
    return (
        plane_table,
        column_table,
        first_table,
        middle_table,
        middle_bias,
        last_weight,
        b_out,
    )


def widen_body(position, own, partner, next_same, next_other, wide):
    orb = position[0]
    wide[pl.ds(HALF * orb, HALF)] = own[...]
    wide[pl.ds(HALF * (1 - orb), HALF)] = partner[...]
    wide[pl.ds(CY + HALF * orb, HALF)] = next_same[...]
    wide[pl.ds(CY + HALF * (1 - orb), HALF)] = next_other[...]


def widen(position, own, partner, next_same, next_other):
    return pl.pallas_call(
        widen_body,
        name="widen_rows",
        out_shape=jax.ShapeDtypeStruct((CY + BOX, CZ, NX), bf16),
        in_specs=[SMEM] + [VMEM] * 4,
        out_specs=VMEM,
        compiler_params=ROOM,
    )(position, own, partner, next_same, next_other)


def cut_body(offsets, wide, beyond, windows, reach):
    reach[:, :CZ, :] = wide[...].astype(f32)
    reach[:, CZ:, :] = beyond[...].astype(f32)
    lane = lanes(BOX)

    def source_step(source, carry):
        mains, tails = [], []
        for slot in range(CAP):
            z0 = offsets[source, 64 * slot]
            y0 = offsets[source, 64 * slot + 1]
            x0 = offsets[source, 64 * slot + 2]
            tiles = [None] * 5
            for b in range(BOX):
                tile, left = divmod(BOX * b, NX)
                piece = reach[y0 + b, pl.ds(z0, BOX), :]
                piece = pltpu.roll(piece, (left - x0) & (NX - 1), 1)
                if tiles[tile] is None:
                    tiles[tile] = piece
                else:
                    tiles[tile] = jnp.where(lane >= left, piece, tiles[tile])
                if left + BOX > NX:
                    tiles[tile + 1] = piece
            mains += tiles[:4]
            tails.append(tiles[4])
        tail = jnp.where(lane < 64, tails[0], pltpu.roll(tails[1], 64, 1))
        windows[source] = jnp.concatenate(mains + [tail], axis=0).astype(bf16)
        return carry

    lax.fori_loop(0, SLABS, source_step, 0)


def cut(offsets, wide, beyond):
    return pl.pallas_call(
        cut_body,
        name="cut_windows",
        out_shape=jax.ShapeDtypeStruct((SLABS, WINDOW_ROWS, NX), bf16),
        in_specs=[SMEM, VMEM, VMEM],
        out_specs=VMEM,
        scratch_shapes=[pltpu.VMEM((CY + BOX, CZ + BOX, NX), f32)],
        compiler_params=ROOM,
    )(offsets, wide, beyond)


def apply_body(corners, windows, orbitals, applied, count):
    def clear(slab, carry):
        count[slab] = 0
        return carry

    lax.fori_loop(0, SLABS, clear, 0)

    def place(i, carry):
        slab = lax.div(corners[0, i], CZ)
        rank = count[slab]
        count[slab] = rank + 1
        main = windows[slab, pl.ds(pl.multiple_of(rank * MAIN, 32), MAIN), :].astype(f32)
        tail = windows[slab, TAIL:WINDOW_ROWS, :].astype(f32)
        tail = jnp.where(rank == 0, tail[:, :64], tail[:, 64:])
        whole = jnp.concatenate([main[BOX * j : BOX * j + BOX] for j in range(4)] + [tail], axis=1)
        applied[i] = (whole * orbitals[i].astype(f32)).astype(bf16)
        return carry

    lax.fori_loop(0, HELD, place, 0)


def apply(corners, windows, orbitals):
    return pl.pallas_call(
        apply_body,
        name="apply_windows",
        out_shape=jax.ShapeDtypeStruct(orbitals.shape, bf16),
        in_specs=[SMEM, VMEM, VMEM],
        out_specs=VMEM,
        scratch_shapes=[pltpu.SMEM((SLABS,), jnp.int32)],
        compiler_params=ROOM,
    )(corners, windows, orbitals)


def exchange(x, axis):
    return lax.all_to_all(x, axis, split_axis=0, concat_axis=0, tiled=True)


def local(orbitals, occupation, corners, kernel_widths, w_in, b_in, w_mid, b_mid, w_out, b_out):
    corners = corners.T
    taps = kernel_taps(kernel_widths)
    tables = model_tables(taps, w_in, b_in, w_mid, b_mid, w_out, b_out)
    received = exchange(pack(corners, occupation, orbitals), "gz")
    position = lax.axis_index("orb").reshape(1)
    own, next_up, second_up, next_down, offsets = deposit(received)
    below = shifted(next_up, "gz", 1)
    second_below = shifted(second_up, "gz", 2)
    above = shifted(next_down, "gz", -1)
    kept, next_right, second_right, next_left = fold_planes(own, below, second_below, above)
    left = crossed(next_right, 1)
    second_left = shifted(second_right, "gy", 2)
    right = crossed(next_left, -1)
    kept, given = fold_rows(position, kept, left, second_left, right)
    half = model(kept, shifted(given, "orb", 1), taps, tables)
    partner = shifted(half, "orb", 1)
    next_same = shifted(half, "gy", -1)
    next_other = crossed(half, -1)
    wide = widen(position, half, partner, next_same, next_other)
    windows = cut(offsets, wide, shifted(wide, "gz", -1))
    applied = apply(corners, exchange(windows, "gz"), orbitals)
    return jnp.transpose(wide[:CY], (1, 0, 2)), applied


def solution(mesh):
    return jax.shard_map(
        local,
        mesh=mesh,
        in_specs=(
            P(("gz", "gy", "orb"), None, None),
            P(("gz", "gy", "orb")),
            P(("gz", "gy", "orb"), None),
            P(),
            P(),
            P(),
            P(),
            P(),
            P(),
            P(),
        ),
        out_specs=(P("gz", "gy", None), P(("gz", "gy", "orb"), None, None)),
        check_vma=False,
    )
```

```python
import jax
import jax.numpy as jnp
from jax import lax
from jax.experimental import pallas as pl
from jax.experimental.pallas import tpu as pltpu
from jax.sharding import PartitionSpec as P

BOX = 24
CHAN = 8
HID = 64
RAD = 6
CZ = 24
CY = 24
NX = 128
CAP = 2
SLABS = 16
HELD = 16
FIRST_PLANE = 10
PLANES = 40
ABOVE = PLANES - CZ
HALF = CY // 2
ROWS = HALF + 2 * RAD
REACH = CY + 2 * RAD
EDGE = REACH // 2
MAIN = 96
TAIL = CAP * MAIN
BLOCK_ROWS = 224
WINDOW_ROWS = TAIL + BOX

VMEM = pl.BlockSpec(memory_space=pltpu.VMEM)
SMEM = pl.BlockSpec(memory_space=pltpu.SMEM)
ROOM = pltpu.CompilerParams(vmem_limit_bytes=16 * 1024 * 1024)
f32 = jnp.float32
bf16 = jnp.bfloat16


def shifted(x, axis, by):
    count = lax.axis_size(axis)
    return lax.ppermute(x, axis, [(i, (i + by) % count) for i in range(count)])


def across_rows(x, steps, cross):
    tiles, owners = lax.axis_size("gy"), lax.axis_size("orb")
    pairs = [
        (tile * owners + orb, (tile + steps[orb]) % tiles * owners + (orb + cross) % owners)
        for tile in range(tiles)
        for orb in range(owners)
    ]
    return lax.ppermute(x, ("gy", "orb"), pairs)


def split(x):
    high = x.astype(bf16)
    return high, (x - high.astype(f32)).astype(bf16)


def split_table(x):
    high = lax.reduce_precision(x, 8, 7)
    return high.astype(bf16), (x - high).astype(bf16)


def lanes(rows):
    return lax.broadcasted_iota(jnp.int32, (rows, NX), 1)


def pack_body(corners, occupation, orbitals, sent, count):
    sent[...] = jnp.zeros(sent.shape, bf16)

    def clear(slab, carry):
        count[slab] = 0
        return carry

    lax.fori_loop(0, SLABS, clear, 0)
    side = lanes(32) // 64
    field = lanes(8) % 64

    def place(i, carry):
        plane = corners[0, i]
        row = corners[1, i]
        column = corners[2, i]
        slab = lax.div(plane, CZ)
        rank = count[slab]
        count[slab] = rank + 1
        values = orbitals[i].astype(f32)
        density = occupation[i] * values * values
        main = jnp.concatenate([density[:, 128 * j : 128 * j + 128] for j in range(4)], axis=0)
        sent[slab, pl.ds(pl.multiple_of(rank * MAIN, 32), MAIN), :] = main.astype(bf16)
        last = density[:, 512:576]
        tail = jnp.concatenate([last, last], axis=1)
        offsets = jnp.where(
            field == 0,
            lax.rem(plane, CZ),
            jnp.where(field == 1, lax.rem(row, CY), jnp.where(field == 2, column, 0)),
        ).astype(f32)
        fresh = jnp.concatenate([tail, offsets], axis=0)
        held = sent[slab, TAIL:BLOCK_ROWS, :].astype(f32)
        sent[slab, TAIL:BLOCK_ROWS, :] = jnp.where(side == rank, fresh, held).astype(bf16)
        return carry

    lax.fori_loop(0, HELD, place, 0)


def pack(corners, occupation, orbitals):
    return pl.pallas_call(
        pack_body,
        name="pack_boxes",
        out_shape=jax.ShapeDtypeStruct((SLABS, BLOCK_ROWS, NX), bf16),
        in_specs=[SMEM, SMEM, VMEM],
        out_specs=VMEM,
        scratch_shapes=[pltpu.SMEM((SLABS,), jnp.int32)],
        compiler_params=ROOM,
    )(corners, occupation, orbitals)


def read_offsets(received, rows, offsets, sem):
    for source in range(SLABS):
        rows[source : source + 1, :] = (
            received[source, 208:BLOCK_ROWS, :].astype(f32)[8:9].astype(jnp.int32)
        )
    copy = pltpu.make_async_copy(rows, offsets, sem)
    copy.start()
    return copy


def deposit_body(received, own, next_up, next_down, offsets_out, grid, rows, offsets, sem):
    copy = read_offsets(received, rows, offsets, sem)
    offsets_out[...] = rows[...]
    grid[...] = jnp.zeros(grid.shape, f32)
    copy.wait()
    lane = lanes(BOX)

    def source_step(source, carry):
        tail_both = received[source, TAIL:BLOCK_ROWS, :].astype(f32)[:BOX]
        for slot in range(CAP):
            z0 = offsets[source, 64 * slot]
            y0 = offsets[source, 64 * slot + 1]
            x0 = offsets[source, 64 * slot + 2]
            main = received[source, MAIN * slot : MAIN * slot + MAIN, :].astype(f32)
            tiles = [main[BOX * j : BOX * j + BOX] for j in range(4)]
            tiles.append(tail_both if slot == 0 else pltpu.roll(tail_both, 64, 1))
            inside = ((lane - x0) & (NX - 1)) < BOX
            for first in range(0, BOX, 8):
                olds = [
                    grid[y0 + b, pl.ds(z0, BOX), :] for b in range(first, first + 8)
                ]
                news = []
                for k in range(8):
                    b = first + k
                    tile, left = divmod(BOX * b, NX)
                    piece = tiles[tile]
                    if left + BOX > NX:
                        piece = jnp.where(lane >= left, piece, tiles[tile + 1])
                    piece = pltpu.roll(piece, (x0 - left) & (NX - 1), 1)
                    news.append(olds[k] + jnp.where(inside, piece, 0.0))
                for k in range(8):
                    grid[y0 + first + k, pl.ds(z0, BOX), :] = news[k]
        return carry

    lax.fori_loop(0, SLABS, source_step, 0)
    own[...] = grid[:, :PLANES, :]
    next_up[...] = grid[:, CZ:, :].astype(bf16)
    next_down[...] = grid[:, :ABOVE, :].astype(bf16)


def deposit(received):
    return pl.pallas_call(
        deposit_body,
        name="deposit_boxes",
        out_shape=(
            jax.ShapeDtypeStruct((CY + BOX, PLANES, NX), f32),
            jax.ShapeDtypeStruct((CY + BOX, BOX, NX), bf16),
            jax.ShapeDtypeStruct((CY + BOX, ABOVE, NX), bf16),
            jax.ShapeDtypeStruct((SLABS, NX), jnp.int32),
        ),
        in_specs=[VMEM],
        out_specs=(VMEM,) * 4,
        scratch_shapes=[
            pltpu.VMEM((CY + BOX, CZ + BOX, NX), f32),
            pltpu.VMEM((SLABS, NX), jnp.int32),
            pltpu.SMEM((SLABS, NX), jnp.int32),
            pltpu.SemaphoreType.DMA,
        ],
        compiler_params=ROOM,
    )(received)


def fold_planes_body(own, below, above, kept, next_right, next_left):
    for first, last in ((0, CZ), (CZ, PLANES)):
        other = below[...] if first == 0 else above[...]
        total = own[:, first:last, :] + other.astype(f32)
        kept[:, first:last, :] = total[RAD : RAD + REACH]
        next_right[:, first:last, :] = total[2 * CY - EDGE :].astype(bf16)
        next_left[:, first:last, :] = total[:EDGE].astype(bf16)


def fold_planes(own, below, above):
    return pl.pallas_call(
        fold_planes_body,
        name="fold_planes",
        out_shape=(
            jax.ShapeDtypeStruct((REACH, PLANES, NX), f32),
            jax.ShapeDtypeStruct((EDGE, PLANES, NX), bf16),
            jax.ShapeDtypeStruct((EDGE, PLANES, NX), bf16),
        ),
        in_specs=[VMEM] * 3,
        out_specs=(VMEM,) * 3,
        compiler_params=ROOM,
    )(own, below, above)


def fold_rows_body(position, own, left, right, kept, given, total):
    total[:EDGE] = own[:EDGE] + left[...].astype(f32)
    total[EDGE:] = own[EDGE:] + right[...].astype(f32)
    orb = position[0]
    kept[...] = total[pl.ds(HALF * orb, ROWS)]
    given[...] = total[pl.ds(HALF * (1 - orb), ROWS)].astype(bf16)


def fold_rows(position, own, left, right):
    return pl.pallas_call(
        fold_rows_body,
        name="fold_rows",
        out_shape=(
            jax.ShapeDtypeStruct((ROWS, PLANES, NX), f32),
            jax.ShapeDtypeStruct((ROWS, PLANES, NX), bf16),
        ),
        in_specs=[SMEM] + [VMEM] * 3,
        out_specs=(VMEM, VMEM),
        scratch_shapes=[pltpu.VMEM((REACH, PLANES, NX), f32)],
        compiler_params=ROOM,
    )(position, own, left, right)


def model_body(
    taps,
    kept,
    other,
    plane_table,
    column_table,
    first_table,
    middle_table,
    middle_bias,
    last_weight,
    last_bias,
    potential,
    planes,
    features,
    result,
):
    def plane_step(pair, carry):
        density = kept[pl.ds(2 * pair, 2)] + other[pl.ds(2 * pair, 2)].astype(f32)
        density = density.astype(bf16)
        field = jnp.concatenate([density[0], density[1]], axis=1)
        both = jnp.dot(plane_table[...], field, preferred_element_type=f32)
        total = both[: CHAN * CZ] + both[CHAN * CZ :]
        planes[2 * pair] = total[:, :NX]
        planes[2 * pair + 1] = total[:, NX:]
        return carry

    lax.fori_loop(0, ROWS // 2, plane_step, 0, unroll=4)

    def channel_step(channel, carry):
        weights = [taps[channel, step] for step in range(RAD + 1)]
        lines = []
        for part in range(CZ // 8):
            start = pl.multiple_of(channel * CZ + 8 * part, 8)
            rows = [planes[y, pl.ds(start, 8), :] for y in range(ROWS)]
            for y in range(HALF):
                total = weights[RAD] * rows[y + RAD]
                for step in range(RAD):
                    total = total + weights[step] * (rows[y + step] + rows[y + 2 * RAD - step])
                lines.append(total)
        high, low = split(jnp.concatenate(lines, axis=0))
        both = jnp.dot(
            jnp.concatenate([high, low], axis=1), column_table[channel], preferred_element_type=f32
        )
        smooth = both[:, :NX] + both[:, NX:]
        features[channel] = jnp.log(1.0 + smooth)
        return carry

    lax.fori_loop(0, CHAN, channel_step, 0, unroll=2)

    def cell_step(step, carry):
        start = pl.multiple_of(step * 16, 16)
        inputs = [features[channel, pl.ds(start, 16), :] for channel in range(CHAN)]
        cells = jnp.concatenate(
            [
                jnp.concatenate([piece[:8] for piece in inputs], axis=0),
                jnp.concatenate([piece[8:] for piece in inputs], axis=0),
            ],
            axis=1,
        )
        high, low = split(cells)
        ones = jnp.ones((16, 2 * NX), bf16)
        stacked = jnp.concatenate([high, low, high, ones], axis=0)
        values = []
        for half in range(2):
            hidden = jnp.dot(
                first_table[256 * half : 256 * half + 256, :], stacked, preferred_element_type=f32
            )
            hidden = hidden + hidden * jnp.tanh(hidden)
            hidden_high, hidden_low = split(hidden)
            for pair in range(2):
                rows = slice(128 * pair, 128 * pair + 128)
                both = jnp.dot(
                    middle_table[...],
                    jnp.concatenate([hidden_high[rows], hidden_low[rows]], axis=0),
                    preferred_element_type=f32,
                )
                mixed = both[:128] + both[128:] + middle_bias[...]
                mixed = (mixed + mixed * jnp.tanh(mixed)) * last_weight[...]
                values.append(jnp.sum(mixed.reshape(2, HID, 2 * NX), axis=1))
        value = jnp.concatenate(values, axis=0) + last_bias[0]
        result[pl.ds(start, 8), :] = value[:, :NX]
        result[pl.ds(start + 8, 8), :] = value[:, NX:]
        return carry

    lax.fori_loop(0, CZ * HALF // 16, cell_step, 0, unroll=9)
    for part in range(CZ // 8):
        block = result[HALF * 8 * part : HALF * 8 * (part + 1), :]
        planes[:HALF, 8 * part : 8 * part + 8, :] = block.reshape(HALF, 8, NX)
    potential[...] = planes[:HALF, :CZ, :].astype(bf16)


def model(kept, other, taps, tables):
    return pl.pallas_call(
        model_body,
        name="smooth_and_network",
        out_shape=jax.ShapeDtypeStruct((HALF, CZ, NX), bf16),
        in_specs=[SMEM] + [VMEM] * 8 + [SMEM],
        out_specs=VMEM,
        scratch_shapes=[
            pltpu.VMEM((ROWS, CHAN * CZ, NX), f32),
            pltpu.VMEM((CHAN, HALF * CZ, NX), f32),
            pltpu.VMEM((HALF * CZ, NX), f32),
        ],
        compiler_params=ROOM,
    )(taps, kept, other, *tables)


def kernel_taps(kernel_widths):
    offsets = jnp.arange(-RAD, RAD + 1).astype(f32)
    raw = jnp.exp(-(offsets[None, :] ** 2) / (2.0 * kernel_widths[:, None] ** 2))
    return raw / jnp.sum(raw, axis=1, keepdims=True)


def tap_table(taps, distance):
    table = jnp.zeros((taps.shape[0],) + distance.shape, f32)
    for step in range(2 * RAD + 1):
        table = table + taps[:, step][:, None, None] * (distance == step).astype(f32)[None]
    return table


def model_tables(taps, w_in, b_in, w_mid, b_mid, w_out, b_out):
    out_index = jnp.arange(CZ, dtype=jnp.int32)
    in_index = jnp.arange(PLANES, dtype=jnp.int32) - (FIRST_PLANE - RAD)
    plane = tap_table(taps, in_index[None, :] - out_index[:, None]).reshape(CHAN * CZ, PLANES)
    plane_table = jnp.concatenate(split_table(plane), axis=0)
    source = jnp.arange(NX, dtype=jnp.int32)
    column = tap_table(taps, (source[:, None] - source[None, :] + RAD) % NX)
    column_high, column_low = split_table(column)
    column_table = jnp.concatenate(
        [
            jnp.concatenate([column_high, column_low], axis=2),
            jnp.concatenate([column_high, jnp.zeros_like(column_low)], axis=2),
        ],
        axis=1,
    )
    eight = jnp.eye(8, dtype=f32)
    first = (0.5 * w_in.T)[None, :, :, None] * eight[:, None, None, :]
    first_high, first_low = split_table(first.reshape(8 * HID, CHAN * 8))
    bias_high, bias_low = split_table(jnp.tile(0.5 * b_in, 8)[:, None])
    first_table = jnp.concatenate(
        [
            first_high,
            first_high,
            first_low,
            bias_high,
            bias_low,
            jnp.zeros((8 * HID, 14), bf16),
        ],
        axis=1,
    )
    two = jnp.eye(2, dtype=f32)
    middle = (two[:, None, :, None] * (0.5 * w_mid.T)[None, :, None, :]).reshape(2 * HID, 2 * HID)
    middle_high, middle_low = split_table(middle)
    middle_table = jnp.concatenate(
        [
            jnp.concatenate([middle_high, middle_high], axis=1),
            jnp.concatenate([middle_low, jnp.zeros_like(middle_low)], axis=1),
        ],
        axis=0,
    )
    middle_bias = jnp.broadcast_to(jnp.tile(0.5 * b_mid, 2)[:, None], (2 * HID, 2 * NX))
    last_weight = jnp.broadcast_to(jnp.tile(w_out, 2)[:, None], (2 * HID, 2 * NX))
    return (
        plane_table,
        column_table,
        first_table,
        middle_table,
        middle_bias,
        last_weight,
        b_out,
    )


def widen_body(position, own, partner, near, far, wide, first_planes, last_planes):
    orb = position[0]
    wide[pl.ds(HALF + HALF * orb, HALF)] = own[...]
    wide[pl.ds(2 * HALF - HALF * orb, HALF)] = partner[...]
    wide[pl.ds(3 * HALF * orb, HALF)] = near[...]
    wide[pl.ds(3 * HALF - 3 * HALF * orb, HALF)] = far[...]
    first_planes[...] = wide[:, :16, :]
    last_planes[...] = wide[...].astype(f32)[:, CZ - 16 :, :].astype(bf16)


def widen(position, own, partner, near, far):
    return pl.pallas_call(
        widen_body,
        name="widen_rows",
        out_shape=(
            jax.ShapeDtypeStruct((CY + BOX, CZ, NX), bf16),
            jax.ShapeDtypeStruct((CY + BOX, 16, NX), bf16),
            jax.ShapeDtypeStruct((CY + BOX, 16, NX), bf16),
        ),
        in_specs=[SMEM] + [VMEM] * 4,
        out_specs=(VMEM,) * 3,
        compiler_params=ROOM,
    )(position, own, partner, near, far)


def cut_body(offsets, wide, below, above, windows, reach):
    reach[:, :FIRST_PLANE, :] = below[...].astype(f32)[:, 16 - FIRST_PLANE :, :]
    reach[:, FIRST_PLANE : FIRST_PLANE + CZ, :] = wide[...].astype(f32)
    reach[:, FIRST_PLANE + CZ :, :] = above[...].astype(f32)[:, : BOX - FIRST_PLANE, :]
    lane = lanes(BOX)

    def source_step(source, carry):
        mains, tails = [], []
        for slot in range(CAP):
            z0 = offsets[source, 64 * slot]
            y0 = offsets[source, 64 * slot + 1]
            x0 = offsets[source, 64 * slot + 2]
            tiles = [None] * 5
            for b in range(BOX):
                tile, left = divmod(BOX * b, NX)
                piece = reach[y0 + b, pl.ds(z0, BOX), :]
                piece = pltpu.roll(piece, (left - x0) & (NX - 1), 1)
                if tiles[tile] is None:
                    tiles[tile] = piece
                else:
                    tiles[tile] = jnp.where(lane >= left, piece, tiles[tile])
                if left + BOX > NX:
                    tiles[tile + 1] = piece
            mains += tiles[:4]
            tails.append(tiles[4])
        tail = jnp.where(lane < 64, tails[0], pltpu.roll(tails[1], 64, 1))
        windows[source] = jnp.concatenate(mains + [tail], axis=0).astype(bf16)
        return carry

    lax.fori_loop(0, SLABS, source_step, 0)


def cut(offsets, wide, below, above):
    return pl.pallas_call(
        cut_body,
        name="cut_windows",
        out_shape=jax.ShapeDtypeStruct((SLABS, WINDOW_ROWS, NX), bf16),
        in_specs=[SMEM, VMEM, VMEM, VMEM],
        out_specs=VMEM,
        scratch_shapes=[pltpu.VMEM((CY + BOX, CZ + BOX, NX), f32)],
        compiler_params=ROOM,
    )(offsets, wide, below, above)


def apply_body(corners, windows, orbitals, applied, count):
    def clear(slab, carry):
        count[slab] = 0
        return carry

    lax.fori_loop(0, SLABS, clear, 0)

    def place(i, carry):
        slab = lax.div(corners[0, i], CZ)
        rank = count[slab]
        count[slab] = rank + 1
        main = windows[slab, pl.ds(pl.multiple_of(rank * MAIN, 32), MAIN), :].astype(f32)
        tail = windows[slab, TAIL:WINDOW_ROWS, :].astype(f32)
        tail = jnp.where(rank == 0, tail[:, :64], tail[:, 64:])
        whole = jnp.concatenate([main[BOX * j : BOX * j + BOX] for j in range(4)] + [tail], axis=1)
        applied[i] = (whole * orbitals[i].astype(f32)).astype(bf16)
        return carry

    lax.fori_loop(0, HELD, place, 0)


def apply(corners, windows, orbitals):
    return pl.pallas_call(
        apply_body,
        name="apply_windows",
        out_shape=jax.ShapeDtypeStruct(orbitals.shape, bf16),
        in_specs=[SMEM, VMEM, VMEM],
        out_specs=VMEM,
        scratch_shapes=[pltpu.SMEM((SLABS,), jnp.int32)],
        compiler_params=ROOM,
    )(corners, windows, orbitals)


def exchange(x, axis):
    return lax.all_to_all(x, axis, split_axis=0, concat_axis=0, tiled=True)


def local(orbitals, occupation, corners, kernel_widths, w_in, b_in, w_mid, b_mid, w_out, b_out):
    corners = corners.T
    taps = kernel_taps(kernel_widths)
    tables = model_tables(taps, w_in, b_in, w_mid, b_mid, w_out, b_out)
    received = exchange(pack(corners, occupation, orbitals), "gz")
    position = lax.axis_index("orb").reshape(1)
    own, next_up, next_down, offsets = deposit(received)
    kept, next_right, next_left = fold_planes(
        own, shifted(next_up, "gz", 1), shifted(next_down, "gz", -1)
    )
    left = across_rows(next_right, (1, 1), 1)
    right = across_rows(next_left, (-1, -1), 1)
    kept, given = fold_rows(position, kept, left, right)
    half = model(kept, shifted(given, "orb", 1), taps, tables)
    partner = shifted(half, "orb", 1)
    near = across_rows(half, (-1, 1), 1)
    far = across_rows(half, (-1, 1), 0)
    wide, first_planes, last_planes = widen(position, half, partner, near, far)
    below = shifted(last_planes, "gz", 1)
    above = shifted(first_planes, "gz", -1)
    windows = cut(offsets, wide, below, above)
    applied = apply(corners, exchange(windows, "gz"), orbitals)
    tile = jnp.concatenate([below[:CY, 16 - FIRST_PLANE :], wide[:CY, : CZ - FIRST_PLANE]], axis=1)
    return jnp.transpose(tile, (1, 0, 2)), applied


def solution(mesh):
    return jax.shard_map(
        local,
        mesh=mesh,
        in_specs=(
            P(("gz", "gy", "orb"), None, None),
            P(("gz", "gy", "orb")),
            P(("gz", "gy", "orb"), None),
            P(),
            P(),
            P(),
            P(),
            P(),
            P(),
            P(),
        ),
        out_specs=(P("gz", "gy", None), P(("gz", "gy", "orb"), None, None)),
        check_vma=False,
    )
```

```python
import jax
import jax.numpy as jnp
from jax import lax
from jax.experimental import pallas as pl
from jax.experimental.pallas import tpu as pltpu
from jax.sharding import PartitionSpec as P

BOX = 24
CHAN = 8
HID = 64
RAD = 6
CZ = 24
CY = 24
NX = 128
CAP = 2
SLABS = 16
HELD = 16
FIRST_PLANE = 10
PLANES = 40
ABOVE = PLANES - CZ
HALF = CY // 2
ROWS = HALF + 2 * RAD
REACH = CY + 2 * RAD
EDGE = REACH // 2
MAIN = 96
TAIL = CAP * MAIN
BLOCK_ROWS = 224
GROUP = 4
WINDOW_ROWS = TAIL + BOX

VMEM = pl.BlockSpec(memory_space=pltpu.VMEM)
SMEM = pl.BlockSpec(memory_space=pltpu.SMEM)
ROOM = pltpu.CompilerParams(vmem_limit_bytes=16 * 1024 * 1024)
f32 = jnp.float32
bf16 = jnp.bfloat16


def shifted(x, axis, by):
    count = lax.axis_size(axis)
    return lax.ppermute(x, axis, [(i, (i + by) % count) for i in range(count)])


def across_rows(x, steps, cross):
    tiles, owners = lax.axis_size("gy"), lax.axis_size("orb")
    pairs = [
        (tile * owners + orb, (tile + steps[orb]) % tiles * owners + (orb + cross) % owners)
        for tile in range(tiles)
        for orb in range(owners)
    ]
    return lax.ppermute(x, ("gy", "orb"), pairs)


def split(x):
    high = x.astype(bf16)
    return high, (x - high.astype(f32)).astype(bf16)


def split_table(x):
    high = lax.reduce_precision(x, 8, 7)
    return high.astype(bf16), (x - high).astype(bf16)


def lanes(rows):
    return lax.broadcasted_iota(jnp.int32, (rows, NX), 1)


def pack_body(corners, occupation, orbitals, sent, boxes, count, sems):
    copies = [pltpu.make_async_copy(orbitals.at[i], boxes.at[i], sems.at[i]) for i in range(HELD)]
    for copy in copies:
        copy.start()
    sent[...] = jnp.zeros(sent.shape, bf16)

    def clear(slab, carry):
        count[slab] = 0
        return carry

    lax.fori_loop(0, SLABS, clear, 0)
    side = lanes(32) // 64
    field = lanes(8) % 64

    def place(i):
        plane = corners[0, i]
        row = corners[1, i]
        column = corners[2, i]
        slab = lax.div(plane, CZ)
        rank = count[slab]
        count[slab] = rank + 1
        values = boxes[i].astype(f32)
        density = occupation[i] * values * values
        main = jnp.concatenate([density[:, 128 * j : 128 * j + 128] for j in range(4)], axis=0)
        sent[slab, pl.ds(pl.multiple_of(rank * MAIN, 32), MAIN), :] = main.astype(bf16)
        last = density[:, 512:576]
        tail = jnp.concatenate([last, last], axis=1)
        offsets = jnp.where(
            field == 0,
            lax.rem(plane, CZ),
            jnp.where(field == 1, lax.rem(row, CY), jnp.where(field == 2, column, 0)),
        ).astype(f32)
        fresh = jnp.concatenate([tail, offsets], axis=0)
        held = sent[slab, TAIL:BLOCK_ROWS, :].astype(f32)
        sent[slab, TAIL:BLOCK_ROWS, :] = jnp.where(side == rank, fresh, held).astype(bf16)

    for i in range(HELD):
        copies[i].wait()
        place(i)


def pack(corners, occupation, orbitals):
    return pl.pallas_call(
        pack_body,
        name="pack_boxes",
        out_shape=jax.ShapeDtypeStruct((SLABS, BLOCK_ROWS, NX), bf16),
        in_specs=[SMEM, SMEM, pl.BlockSpec(memory_space=pl.ANY)],
        out_specs=VMEM,
        scratch_shapes=[
            pltpu.VMEM((HELD, BOX, BOX * BOX), bf16),
            pltpu.SMEM((SLABS,), jnp.int32),
            pltpu.SemaphoreType.DMA((HELD,)),
        ],
        compiler_params=pltpu.CompilerParams(vmem_limit_bytes=60 * 1024 * 1024),
    )(corners, occupation, orbitals)


def read_offsets(received, rows, offsets, sem):
    for source in range(SLABS):
        rows[source : source + 1, :] = (
            received[source, 208:BLOCK_ROWS, :].astype(f32)[8:9].astype(jnp.int32)
        )
    copy = pltpu.make_async_copy(rows, offsets, sem)
    copy.start()
    return copy


def deposit_body(received, own, next_up, next_down, offsets_out, grids, rows, offsets, sem):
    copy = read_offsets(received, rows, offsets, sem)
    offsets_out[...] = rows[...]
    for grid in grids:
        grid[...] = jnp.zeros(grid.shape, f32)
    copy.wait()
    lane = lanes(BOX)

    def source_step(source, carry):
        tail_both = received[source, TAIL:BLOCK_ROWS, :].astype(f32)[:BOX]
        boxes = []
        for slot in range(CAP):
            start = [offsets[source, 64 * slot + field] for field in range(3)]
            main = received[source, MAIN * slot : MAIN * slot + MAIN, :].astype(f32)
            tiles = [main[BOX * j : BOX * j + BOX] for j in range(4)]
            tiles.append(tail_both if slot == 0 else pltpu.roll(tail_both, 64, 1))
            boxes.append((start, tiles, ((lane - start[2]) & (NX - 1)) < BOX))
        for first in range(0, BOX, GROUP):
            for slot in range(CAP):
                (z0, y0, x0), tiles, inside = boxes[slot]
                grid = grids[slot]
                olds = [grid[y0 + first + k, pl.ds(z0, BOX), :] for k in range(GROUP)]
                news = []
                for k in range(GROUP):
                    tile, left = divmod(BOX * (first + k), NX)
                    piece = tiles[tile]
                    if left + BOX > NX:
                        piece = jnp.where(lane >= left, piece, tiles[tile + 1])
                    piece = pltpu.roll(piece, (x0 - left) & (NX - 1), 1)
                    news.append(olds[k] + jnp.where(inside, piece, 0.0))
                for k in range(GROUP):
                    grid[y0 + first + k, pl.ds(z0, BOX), :] = news[k]
        return carry

    lax.fori_loop(0, SLABS, source_step, 0)
    own[...] = grids[0][:, :PLANES, :] + grids[1][:, :PLANES, :]
    next_up[...] = (grids[0][:, CZ:, :] + grids[1][:, CZ:, :]).astype(bf16)
    next_down[...] = (grids[0][:, :ABOVE, :] + grids[1][:, :ABOVE, :]).astype(bf16)


def deposit(received):
    return pl.pallas_call(
        deposit_body,
        name="deposit_boxes",
        out_shape=(
            jax.ShapeDtypeStruct((CY + BOX, PLANES, NX), f32),
            jax.ShapeDtypeStruct((CY + BOX, BOX, NX), bf16),
            jax.ShapeDtypeStruct((CY + BOX, ABOVE, NX), bf16),
            jax.ShapeDtypeStruct((SLABS, NX), jnp.int32),
        ),
        in_specs=[VMEM],
        out_specs=(VMEM,) * 4,
        scratch_shapes=[
            [pltpu.VMEM((CY + BOX, CZ + BOX, NX), f32)] * CAP,
            pltpu.VMEM((SLABS, NX), jnp.int32),
            pltpu.SMEM((SLABS, NX), jnp.int32),
            pltpu.SemaphoreType.DMA,
        ],
        compiler_params=ROOM,
    )(received)


def fold_planes_body(own, below, above, kept, next_right, next_left):
    for first, last in ((0, CZ), (CZ, PLANES)):
        other = below[...] if first == 0 else above[...]
        total = own[:, first:last, :] + other.astype(f32)
        kept[:, first:last, :] = total[RAD : RAD + REACH]
        next_right[:, first:last, :] = total[2 * CY - EDGE :].astype(bf16)
        next_left[:, first:last, :] = total[:EDGE].astype(bf16)


def fold_planes(own, below, above):
    return pl.pallas_call(
        fold_planes_body,
        name="fold_planes",
        out_shape=(
            jax.ShapeDtypeStruct((REACH, PLANES, NX), f32),
            jax.ShapeDtypeStruct((EDGE, PLANES, NX), bf16),
            jax.ShapeDtypeStruct((EDGE, PLANES, NX), bf16),
        ),
        in_specs=[VMEM] * 3,
        out_specs=(VMEM,) * 3,
        compiler_params=ROOM,
    )(own, below, above)


def fold_rows_body(position, own, left, right, kept, given, total):
    total[:EDGE] = own[:EDGE] + left[...].astype(f32)
    total[EDGE:] = own[EDGE:] + right[...].astype(f32)
    orb = position[0]
    kept[...] = total[pl.ds(HALF * orb, ROWS)]
    given[...] = total[pl.ds(HALF * (1 - orb), ROWS)].astype(bf16)


def fold_rows(position, own, left, right):
    return pl.pallas_call(
        fold_rows_body,
        name="fold_rows",
        out_shape=(
            jax.ShapeDtypeStruct((ROWS, PLANES, NX), f32),
            jax.ShapeDtypeStruct((ROWS, PLANES, NX), bf16),
        ),
        in_specs=[SMEM] + [VMEM] * 3,
        out_specs=(VMEM, VMEM),
        scratch_shapes=[pltpu.VMEM((REACH, PLANES, NX), f32)],
        compiler_params=ROOM,
    )(position, own, left, right)


def model_body(
    taps,
    kept,
    other,
    plane_table,
    column_table,
    first_table,
    middle_table,
    middle_bias,
    last_weight,
    last_bias,
    potential,
    planes,
    features,
    result,
):
    def plane_step(pair, carry):
        density = kept[pl.ds(2 * pair, 2)] + other[pl.ds(2 * pair, 2)].astype(f32)
        density = density.astype(bf16)
        field = jnp.concatenate([density[0], density[1]], axis=1)
        both = jnp.dot(plane_table[...], field, preferred_element_type=f32)
        total = both[: CHAN * CZ] + both[CHAN * CZ :]
        planes[2 * pair] = total[:, :NX]
        planes[2 * pair + 1] = total[:, NX:]
        return carry

    lax.fori_loop(0, ROWS // 2, plane_step, 0, unroll=4)

    def channel_step(channel, carry):
        weights = [taps[channel, step] for step in range(RAD + 1)]
        lines = []
        for part in range(CZ // 8):
            start = pl.multiple_of(channel * CZ + 8 * part, 8)
            rows = [planes[y, pl.ds(start, 8), :] for y in range(ROWS)]
            for y in range(HALF):
                total = weights[RAD] * rows[y + RAD]
                for step in range(RAD):
                    total = total + weights[step] * (rows[y + step] + rows[y + 2 * RAD - step])
                lines.append(total)
        high, low = split(jnp.concatenate(lines, axis=0))
        both = jnp.dot(
            jnp.concatenate([high, low], axis=1), column_table[channel], preferred_element_type=f32
        )
        smooth = both[:, :NX] + both[:, NX:]
        features[channel] = jnp.log(1.0 + smooth)
        return carry

    lax.fori_loop(0, CHAN, channel_step, 0, unroll=2)

    def cell_step(step, carry):
        start = pl.multiple_of(step * 16, 16)
        inputs = [features[channel, pl.ds(start, 16), :] for channel in range(CHAN)]
        cells = jnp.concatenate(
            [
                jnp.concatenate([piece[:8] for piece in inputs], axis=0),
                jnp.concatenate([piece[8:] for piece in inputs], axis=0),
            ],
            axis=1,
        )
        high, low = split(cells)
        ones = jnp.ones((16, 2 * NX), bf16)
        stacked = jnp.concatenate([high, low, high, ones], axis=0)
        values = []
        for half in range(2):
            hidden = jnp.dot(
                first_table[256 * half : 256 * half + 256, :], stacked, preferred_element_type=f32
            )
            hidden = hidden + hidden * jnp.tanh(hidden)
            hidden_high, hidden_low = split(hidden)
            for pair in range(2):
                rows = slice(128 * pair, 128 * pair + 128)
                both = jnp.dot(
                    middle_table[...],
                    jnp.concatenate([hidden_high[rows], hidden_low[rows]], axis=0),
                    preferred_element_type=f32,
                )
                mixed = both[:128] + both[128:] + middle_bias[...]
                mixed = (mixed + mixed * jnp.tanh(mixed)) * last_weight[...]
                values.append(jnp.sum(mixed.reshape(2, HID, 2 * NX), axis=1))
        value = jnp.concatenate(values, axis=0) + last_bias[0]
        result[pl.ds(start, 8), :] = value[:, :NX]
        result[pl.ds(start + 8, 8), :] = value[:, NX:]
        return carry

    lax.fori_loop(0, CZ * HALF // 16, cell_step, 0, unroll=9)
    for part in range(CZ // 8):
        block = result[HALF * 8 * part : HALF * 8 * (part + 1), :]
        planes[:HALF, 8 * part : 8 * part + 8, :] = block.reshape(HALF, 8, NX)
    potential[...] = planes[:HALF, :CZ, :].astype(bf16)


def model(kept, other, taps, tables):
    return pl.pallas_call(
        model_body,
        name="smooth_and_network",
        out_shape=jax.ShapeDtypeStruct((HALF, CZ, NX), bf16),
        in_specs=[SMEM] + [VMEM] * 8 + [SMEM],
        out_specs=VMEM,
        scratch_shapes=[
            pltpu.VMEM((ROWS, CHAN * CZ, NX), f32),
            pltpu.VMEM((CHAN, HALF * CZ, NX), f32),
            pltpu.VMEM((HALF * CZ, NX), f32),
        ],
        compiler_params=ROOM,
    )(taps, kept, other, *tables)


def tap_weights(kernel_widths, distance):
    width = kernel_widths.reshape((CHAN,) + (1,) * distance.ndim)
    reach = jnp.arange(-RAD, RAD + 1).astype(f32).reshape((2 * RAD + 1,) + (1,) * distance.ndim)
    whole = jnp.sum(jnp.exp(-(reach**2)[None] / (2.0 * width[:, None] ** 2)), axis=1)
    far = distance.astype(f32)[None]
    raw = jnp.where(jnp.abs(far) <= RAD, jnp.exp(-(far**2) / (2.0 * width**2)), 0.0)
    return raw / whole


def model_tables(kernel_widths, w_in, b_in, w_mid, b_mid, w_out, b_out):
    out_index = jnp.arange(CZ, dtype=jnp.int32)
    in_index = jnp.arange(PLANES, dtype=jnp.int32) - FIRST_PLANE
    plane = tap_weights(kernel_widths, in_index[None, :] - out_index[:, None])
    plane = plane.reshape(CHAN * CZ, PLANES)
    plane_table = jnp.concatenate(split_table(plane), axis=0)
    source = jnp.arange(NX, dtype=jnp.int32)
    around = (source[:, None] - source[None, :] + NX // 2) % NX - NX // 2
    column = tap_weights(kernel_widths, around)
    column_high, column_low = split_table(column)
    column_table = jnp.concatenate(
        [
            jnp.concatenate([column_high, column_low], axis=2),
            jnp.concatenate([column_high, jnp.zeros_like(column_low)], axis=2),
        ],
        axis=1,
    )
    eight = jnp.eye(8, dtype=f32)
    first = (0.5 * w_in.T)[None, :, :, None] * eight[:, None, None, :]
    first_high, first_low = split_table(first.reshape(8 * HID, CHAN * 8))
    bias_high, bias_low = split_table(jnp.tile(0.5 * b_in, 8)[:, None])
    first_table = jnp.concatenate(
        [
            first_high,
            first_high,
            first_low,
            bias_high,
            bias_low,
            jnp.zeros((8 * HID, 14), bf16),
        ],
        axis=1,
    )
    two = jnp.eye(2, dtype=f32)
    middle = (two[:, None, :, None] * (0.5 * w_mid.T)[None, :, None, :]).reshape(2 * HID, 2 * HID)
    middle_high, middle_low = split_table(middle)
    middle_table = jnp.concatenate(
        [
            jnp.concatenate([middle_high, middle_high], axis=1),
            jnp.concatenate([middle_low, jnp.zeros_like(middle_low)], axis=1),
        ],
        axis=0,
    )
    middle_bias = jnp.broadcast_to(jnp.tile(0.5 * b_mid, 2)[:, None], (2 * HID, 2 * NX))
    last_weight = jnp.broadcast_to(jnp.tile(w_out, 2)[:, None], (2 * HID, 2 * NX))
    return (
        plane_table,
        column_table,
        first_table,
        middle_table,
        middle_bias,
        last_weight,
        b_out,
    )


def widen_body(position, own, partner, near, far, wide, first_planes, last_planes):
    orb = position[0]
    wide[pl.ds(HALF + HALF * orb, HALF)] = own[...]
    wide[pl.ds(2 * HALF - HALF * orb, HALF)] = partner[...]
    wide[pl.ds(3 * HALF * orb, HALF)] = near[...]
    wide[pl.ds(3 * HALF - 3 * HALF * orb, HALF)] = far[...]
    first_planes[...] = wide[:, :16, :]
    last_planes[...] = wide[...].astype(f32)[:, CZ - 16 :, :].astype(bf16)


def widen(position, own, partner, near, far):
    return pl.pallas_call(
        widen_body,
        name="widen_rows",
        out_shape=(
            jax.ShapeDtypeStruct((CY + BOX, CZ, NX), bf16),
            jax.ShapeDtypeStruct((CY + BOX, 16, NX), bf16),
            jax.ShapeDtypeStruct((CY + BOX, 16, NX), bf16),
        ),
        in_specs=[SMEM] + [VMEM] * 4,
        out_specs=(VMEM,) * 3,
        compiler_params=ROOM,
    )(position, own, partner, near, far)


def cut_body(offsets, wide, below, above, windows, reach):
    reach[:, :FIRST_PLANE, :] = below[...].astype(f32)[:, 16 - FIRST_PLANE :, :]
    reach[:, FIRST_PLANE : FIRST_PLANE + CZ, :] = wide[...].astype(f32)
    reach[:, FIRST_PLANE + CZ :, :] = above[...].astype(f32)[:, : BOX - FIRST_PLANE, :]
    lane = lanes(BOX)

    def source_step(source, carry):
        mains, tails = [], []
        for slot in range(CAP):
            z0 = offsets[source, 64 * slot]
            y0 = offsets[source, 64 * slot + 1]
            x0 = offsets[source, 64 * slot + 2]
            tiles = [None] * 5
            for b in range(BOX):
                tile, left = divmod(BOX * b, NX)
                piece = reach[y0 + b, pl.ds(z0, BOX), :]
                piece = pltpu.roll(piece, (left - x0) & (NX - 1), 1)
                if tiles[tile] is None:
                    tiles[tile] = piece
                else:
                    tiles[tile] = jnp.where(lane >= left, piece, tiles[tile])
                if left + BOX > NX:
                    tiles[tile + 1] = piece
            mains += tiles[:4]
            tails.append(tiles[4])
        tail = jnp.where(lane < 64, tails[0], pltpu.roll(tails[1], 64, 1))
        windows[source] = jnp.concatenate(mains + [tail], axis=0).astype(bf16)
        return carry

    lax.fori_loop(0, SLABS, source_step, 0, unroll=2)


def cut(offsets, wide, below, above):
    return pl.pallas_call(
        cut_body,
        name="cut_windows",
        out_shape=jax.ShapeDtypeStruct((SLABS, WINDOW_ROWS, NX), bf16),
        in_specs=[SMEM, VMEM, VMEM, VMEM],
        out_specs=VMEM,
        scratch_shapes=[pltpu.VMEM((CY + BOX, CZ + BOX, NX), f32)],
        compiler_params=ROOM,
    )(offsets, wide, below, above)


def apply_body(corners, windows, orbitals, applied, count):
    def clear(slab, carry):
        count[slab] = 0
        return carry

    lax.fori_loop(0, SLABS, clear, 0)

    def place(i, carry):
        slab = lax.div(corners[0, i], CZ)
        rank = count[slab]
        count[slab] = rank + 1
        main = windows[slab, pl.ds(pl.multiple_of(rank * MAIN, 32), MAIN), :].astype(f32)
        tail = windows[slab, TAIL:WINDOW_ROWS, :].astype(f32)
        tail = jnp.where(rank == 0, tail[:, :64], tail[:, 64:])
        whole = jnp.concatenate([main[BOX * j : BOX * j + BOX] for j in range(4)] + [tail], axis=1)
        applied[i] = (whole * orbitals[i].astype(f32)).astype(bf16)
        return carry

    lax.fori_loop(0, HELD, place, 0, unroll=4)


def apply(corners, windows, orbitals):
    return pl.pallas_call(
        apply_body,
        name="apply_windows",
        out_shape=jax.ShapeDtypeStruct(orbitals.shape, bf16),
        in_specs=[SMEM, VMEM, VMEM],
        out_specs=VMEM,
        scratch_shapes=[pltpu.SMEM((SLABS,), jnp.int32)],
        compiler_params=ROOM,
    )(corners, windows, orbitals)


def exchange(x, axis):
    return lax.all_to_all(x, axis, split_axis=0, concat_axis=0, tiled=True)


def local(orbitals, occupation, corners, kernel_widths, w_in, b_in, w_mid, b_mid, w_out, b_out):
    corners = corners.T
    taps = tap_weights(kernel_widths, jnp.arange(-RAD, RAD + 1))
    tables = model_tables(kernel_widths, w_in, b_in, w_mid, b_mid, w_out, b_out)
    received = exchange(pack(corners, occupation, orbitals), "gz")
    received, taps, tables = lax.optimization_barrier((received, taps, tables))
    position = lax.axis_index("orb").reshape(1)
    own, next_up, next_down, offsets = deposit(received)
    kept, next_right, next_left = fold_planes(
        own, shifted(next_up, "gz", 1), shifted(next_down, "gz", -1)
    )
    left = across_rows(next_right, (1, 1), 1)
    right = across_rows(next_left, (-1, -1), 1)
    kept, given = fold_rows(position, kept, left, right)
    half = model(kept, shifted(given, "orb", 1), taps, tables)
    partner = shifted(half, "orb", 1)
    near = across_rows(half, (-1, 1), 1)
    far = across_rows(half, (-1, 1), 0)
    wide, first_planes, last_planes = widen(position, half, partner, near, far)
    below = shifted(last_planes, "gz", 1)
    above = shifted(first_planes, "gz", -1)
    windows = cut(offsets, wide, below, above)
    applied = apply(corners, exchange(windows, "gz"), orbitals)
    tile = jnp.concatenate([below[:CY, 16 - FIRST_PLANE :], wide[:CY, : CZ - FIRST_PLANE]], axis=1)
    return jnp.transpose(tile, (1, 0, 2)), applied


def solution(mesh):
    return jax.shard_map(
        local,
        mesh=mesh,
        in_specs=(
            P(("gz", "gy", "orb"), None, None),
            P(("gz", "gy", "orb")),
            P(("gz", "gy", "orb"), None),
            P(),
            P(),
            P(),
            P(),
            P(),
            P(),
            P(),
        ),
        out_specs=(P("gz", "gy", None), P(("gz", "gy", "orb"), None, None)),
        check_vma=False,
    )
```

```python
import jax
import jax.numpy as jnp
from jax import lax
from jax.experimental import pallas as pl
from jax.experimental.pallas import tpu as pltpu
from jax.sharding import PartitionSpec as P

BOX = 24
CHAN = 8
HID = 64
RAD = 6
CZ = 24
CY = 24
NX = 128
CAP = 2
SLABS = 16
HELD = 16
FIRST_PLANE = 10
PLANES = 40
ABOVE = PLANES - CZ
HALF = CY // 2
ROWS = HALF + 2 * RAD
REACH = CY + 2 * RAD
EDGE = REACH // 2
MAIN = 96
TAIL = CAP * MAIN
BLOCK_ROWS = 224
GROUP = 4
PART = 4
WINDOW_ROWS = TAIL + BOX

VMEM = pl.BlockSpec(memory_space=pltpu.VMEM)
SMEM = pl.BlockSpec(memory_space=pltpu.SMEM)
ROOM = pltpu.CompilerParams(vmem_limit_bytes=16 * 1024 * 1024)
f32 = jnp.float32
bf16 = jnp.bfloat16


def shifted(x, axis, by):
    count = lax.axis_size(axis)
    return lax.ppermute(x, axis, [(i, (i + by) % count) for i in range(count)])


def across_rows(x, steps, cross):
    tiles, owners = lax.axis_size("gy"), lax.axis_size("orb")
    pairs = [
        (tile * owners + orb, (tile + steps[orb]) % tiles * owners + (orb + cross) % owners)
        for tile in range(tiles)
        for orb in range(owners)
    ]
    return lax.ppermute(x, ("gy", "orb"), pairs)


def split(x):
    high = x.astype(bf16)
    return high, (x - high.astype(f32)).astype(bf16)


def split_table(x):
    high = lax.reduce_precision(x, 8, 7)
    return high.astype(bf16), (x - high).astype(bf16)


def lanes(rows):
    return lax.broadcasted_iota(jnp.int32, (rows, NX), 1)


def pack_body(corners, occupation, orbitals, sent, boxes, count, sems):
    copies = [
        pltpu.make_async_copy(
            orbitals.at[pl.ds(PART * i, PART)], boxes.at[pl.ds(PART * i, PART)], sems.at[i]
        )
        for i in range(HELD // PART)
    ]
    for copy in copies:
        copy.start()
    sent[...] = jnp.zeros(sent.shape, bf16)

    def clear(slab, carry):
        count[slab] = 0
        return carry

    lax.fori_loop(0, SLABS, clear, 0)
    side = lanes(32) // 64
    field = lanes(8) % 64

    def place(i):
        plane = corners[0, i]
        row = corners[1, i]
        column = corners[2, i]
        slab = lax.div(plane, CZ)
        rank = count[slab]
        count[slab] = rank + 1
        values = boxes[i].astype(f32)
        density = occupation[i] * values * values
        main = jnp.concatenate([density[:, 128 * j : 128 * j + 128] for j in range(4)], axis=0)
        sent[slab, pl.ds(pl.multiple_of(rank * MAIN, 32), MAIN), :] = main.astype(bf16)
        last = density[:, 512:576]
        tail = jnp.concatenate([last, last], axis=1)
        offsets = jnp.where(
            field == 0,
            lax.rem(plane, CZ),
            jnp.where(field == 1, lax.rem(row, CY), jnp.where(field == 2, column, 0)),
        ).astype(f32)
        fresh = jnp.concatenate([tail, offsets], axis=0)
        held = sent[slab, TAIL:BLOCK_ROWS, :].astype(f32)
        sent[slab, TAIL:BLOCK_ROWS, :] = jnp.where(side == rank, fresh, held).astype(bf16)

    for i in range(HELD):
        if i % PART == 0:
            copies[i // PART].wait()
        place(i)


def pack(corners, occupation, orbitals):
    return pl.pallas_call(
        pack_body,
        name="pack_boxes",
        out_shape=jax.ShapeDtypeStruct((SLABS, BLOCK_ROWS, NX), bf16),
        in_specs=[SMEM, SMEM, pl.BlockSpec(memory_space=pl.ANY)],
        out_specs=VMEM,
        scratch_shapes=[
            pltpu.VMEM((HELD, BOX, BOX * BOX), bf16),
            pltpu.SMEM((SLABS,), jnp.int32),
            pltpu.SemaphoreType.DMA((HELD // PART,)),
        ],
        compiler_params=pltpu.CompilerParams(vmem_limit_bytes=60 * 1024 * 1024),
    )(corners, occupation, orbitals)


def read_offsets(received, rows, offsets, sem):
    for source in range(SLABS):
        rows[source : source + 1, :] = (
            received[source, 208:BLOCK_ROWS, :].astype(f32)[8:9].astype(jnp.int32)
        )
    copy = pltpu.make_async_copy(rows, offsets, sem)
    copy.start()
    return copy


def deposit_body(received, own, next_up, next_down, offsets_out, grids, rows, offsets, sem):
    copy = read_offsets(received, rows, offsets, sem)
    offsets_out[...] = rows[...]
    for grid in grids:
        grid[...] = jnp.zeros(grid.shape, f32)
    copy.wait()
    lane = lanes(BOX)

    def source_step(source, carry):
        tail_both = received[source, TAIL:BLOCK_ROWS, :].astype(f32)[:BOX]
        boxes = []
        for slot in range(CAP):
            start = [offsets[source, 64 * slot + field] for field in range(3)]
            main = received[source, MAIN * slot : MAIN * slot + MAIN, :].astype(f32)
            tiles = [main[BOX * j : BOX * j + BOX] for j in range(4)]
            tiles.append(tail_both if slot == 0 else pltpu.roll(tail_both, 64, 1))
            boxes.append((start, tiles, ((lane - start[2]) & (NX - 1)) < BOX))
        for first in range(0, BOX, GROUP):
            for slot in range(CAP):
                (z0, y0, x0), tiles, inside = boxes[slot]
                grid = grids[slot]
                olds = [grid[y0 + first + k, pl.ds(z0, BOX), :] for k in range(GROUP)]
                news = []
                for k in range(GROUP):
                    tile, left = divmod(BOX * (first + k), NX)
                    piece = tiles[tile]
                    if left + BOX > NX:
                        piece = jnp.where(lane >= left, piece, tiles[tile + 1])
                    piece = pltpu.roll(piece, (x0 - left) & (NX - 1), 1)
                    news.append(olds[k] + jnp.where(inside, piece, 0.0))
                for k in range(GROUP):
                    grid[y0 + first + k, pl.ds(z0, BOX), :] = news[k]
        return carry

    lax.fori_loop(0, SLABS, source_step, 0)
    own[...] = grids[0][:, :PLANES, :] + grids[1][:, :PLANES, :]
    next_up[...] = (grids[0][:, CZ:, :] + grids[1][:, CZ:, :]).astype(bf16)
    next_down[...] = (grids[0][:, :ABOVE, :] + grids[1][:, :ABOVE, :]).astype(bf16)


def deposit(received):
    return pl.pallas_call(
        deposit_body,
        name="deposit_boxes",
        out_shape=(
            jax.ShapeDtypeStruct((CY + BOX, PLANES, NX), f32),
            jax.ShapeDtypeStruct((CY + BOX, BOX, NX), bf16),
            jax.ShapeDtypeStruct((CY + BOX, ABOVE, NX), bf16),
            jax.ShapeDtypeStruct((SLABS, NX), jnp.int32),
        ),
        in_specs=[VMEM],
        out_specs=(VMEM,) * 4,
        scratch_shapes=[
            [pltpu.VMEM((CY + BOX, CZ + BOX, NX), f32)] * CAP,
            pltpu.VMEM((SLABS, NX), jnp.int32),
            pltpu.SMEM((SLABS, NX), jnp.int32),
            pltpu.SemaphoreType.DMA,
        ],
        compiler_params=ROOM,
    )(received)


def fold_planes_body(own, below, above, kept, next_right, next_left):
    for first, last in ((0, CZ), (CZ, PLANES)):
        other = below[...] if first == 0 else above[...]
        total = own[:, first:last, :] + other.astype(f32)
        kept[:, first:last, :] = total[RAD : RAD + REACH]
        next_right[:, first:last, :] = total[2 * CY - EDGE :].astype(bf16)
        next_left[:, first:last, :] = total[:EDGE].astype(bf16)


def fold_planes(own, below, above):
    return pl.pallas_call(
        fold_planes_body,
        name="fold_planes",
        out_shape=(
            jax.ShapeDtypeStruct((REACH, PLANES, NX), f32),
            jax.ShapeDtypeStruct((EDGE, PLANES, NX), bf16),
            jax.ShapeDtypeStruct((EDGE, PLANES, NX), bf16),
        ),
        in_specs=[VMEM] * 3,
        out_specs=(VMEM,) * 3,
        compiler_params=ROOM,
    )(own, below, above)


def fold_rows_body(position, own, left, right, kept, given, total):
    total[:EDGE] = own[:EDGE] + left[...].astype(f32)
    total[EDGE:] = own[EDGE:] + right[...].astype(f32)
    orb = position[0]
    kept[...] = total[pl.ds(HALF * orb, ROWS)]
    given[...] = total[pl.ds(HALF * (1 - orb), ROWS)].astype(bf16)


def fold_rows(position, own, left, right):
    return pl.pallas_call(
        fold_rows_body,
        name="fold_rows",
        out_shape=(
            jax.ShapeDtypeStruct((ROWS, PLANES, NX), f32),
            jax.ShapeDtypeStruct((ROWS, PLANES, NX), bf16),
        ),
        in_specs=[SMEM] + [VMEM] * 3,
        out_specs=(VMEM, VMEM),
        scratch_shapes=[pltpu.VMEM((REACH, PLANES, NX), f32)],
        compiler_params=ROOM,
    )(position, own, left, right)


def model_body(
    taps,
    kept,
    other,
    plane_table,
    column_table,
    first_table,
    middle_table,
    middle_bias,
    last_weight,
    last_bias,
    potential,
    planes,
    features,
    result,
):
    def plane_step(pair, carry):
        density = kept[pl.ds(2 * pair, 2)] + other[pl.ds(2 * pair, 2)].astype(f32)
        density = density.astype(bf16)
        field = jnp.concatenate([density[0], density[1]], axis=1)
        both = jnp.dot(plane_table[...], field, preferred_element_type=f32)
        total = both[: CHAN * CZ] + both[CHAN * CZ :]
        planes[2 * pair] = total[:, :NX]
        planes[2 * pair + 1] = total[:, NX:]
        return carry

    lax.fori_loop(0, ROWS // 2, plane_step, 0, unroll=12)

    def channel_step(channel, carry):
        weights = [taps[channel, step] for step in range(RAD + 1)]
        lines = []
        for part in range(CZ // 8):
            start = pl.multiple_of(channel * CZ + 8 * part, 8)
            rows = [planes[y, pl.ds(start, 8), :] for y in range(ROWS)]
            for y in range(HALF):
                total = weights[RAD] * rows[y + RAD]
                for step in range(RAD):
                    total = total + weights[step] * (rows[y + step] + rows[y + 2 * RAD - step])
                lines.append(total)
        high, low = split(jnp.concatenate(lines, axis=0))
        both = jnp.dot(
            jnp.concatenate([high, low], axis=1), column_table[channel], preferred_element_type=f32
        )
        smooth = both[:, :NX] + both[:, NX:]
        features[channel] = jnp.log(1.0 + smooth)
        return carry

    lax.fori_loop(0, CHAN, channel_step, 0, unroll=8)

    def cell_step(step, carry):
        start = pl.multiple_of(step * 16, 16)
        inputs = [features[channel, pl.ds(start, 16), :] for channel in range(CHAN)]
        cells = jnp.concatenate(
            [
                jnp.concatenate([piece[:8] for piece in inputs], axis=0),
                jnp.concatenate([piece[8:] for piece in inputs], axis=0),
            ],
            axis=1,
        )
        high, low = split(cells)
        ones = jnp.ones((16, 2 * NX), bf16)
        stacked = jnp.concatenate([high, low, high, ones], axis=0)
        values = []
        for half in range(2):
            hidden = jnp.dot(
                first_table[256 * half : 256 * half + 256, :], stacked, preferred_element_type=f32
            )
            hidden = hidden + hidden * jnp.tanh(hidden)
            hidden_high, hidden_low = split(hidden)
            for pair in range(2):
                rows = slice(128 * pair, 128 * pair + 128)
                both = jnp.dot(
                    middle_table[...],
                    jnp.concatenate([hidden_high[rows], hidden_low[rows]], axis=0),
                    preferred_element_type=f32,
                )
                mixed = both[:128] + both[128:] + middle_bias[...]
                mixed = (mixed + mixed * jnp.tanh(mixed)) * last_weight[...]
                values.append(jnp.sum(mixed.reshape(2, HID, 2 * NX), axis=1))
        value = jnp.concatenate(values, axis=0) + last_bias[0]
        result[pl.ds(start, 8), :] = value[:, :NX]
        result[pl.ds(start + 8, 8), :] = value[:, NX:]
        return carry

    lax.fori_loop(0, CZ * HALF // 16, cell_step, 0, unroll=9)
    for part in range(CZ // 8):
        block = result[HALF * 8 * part : HALF * 8 * (part + 1), :]
        planes[:HALF, 8 * part : 8 * part + 8, :] = block.reshape(HALF, 8, NX)
    potential[...] = planes[:HALF, :CZ, :].astype(bf16)


def model(kept, other, taps, tables):
    return pl.pallas_call(
        model_body,
        name="smooth_and_network",
        out_shape=jax.ShapeDtypeStruct((HALF, CZ, NX), bf16),
        in_specs=[SMEM] + [VMEM] * 8 + [SMEM],
        out_specs=VMEM,
        scratch_shapes=[
            pltpu.VMEM((ROWS, CHAN * CZ, NX), f32),
            pltpu.VMEM((CHAN, HALF * CZ, NX), f32),
            pltpu.VMEM((HALF * CZ, NX), f32),
        ],
        compiler_params=ROOM,
    )(taps, kept, other, *tables)


def tap_weights(kernel_widths, distance):
    width = kernel_widths.reshape((CHAN,) + (1,) * distance.ndim)
    reach = jnp.arange(-RAD, RAD + 1).astype(f32).reshape((2 * RAD + 1,) + (1,) * distance.ndim)
    whole = jnp.sum(jnp.exp(-(reach**2)[None] / (2.0 * width[:, None] ** 2)), axis=1)
    far = distance.astype(f32)[None]
    raw = jnp.where(jnp.abs(far) <= RAD, jnp.exp(-(far**2) / (2.0 * width**2)), 0.0)
    return raw / whole


def model_tables(kernel_widths, w_in, b_in, w_mid, b_mid, w_out, b_out):
    out_index = jnp.arange(CZ, dtype=jnp.int32)
    in_index = jnp.arange(PLANES, dtype=jnp.int32) - FIRST_PLANE
    plane = tap_weights(kernel_widths, in_index[None, :] - out_index[:, None])
    plane = plane.reshape(CHAN * CZ, PLANES)
    plane_table = jnp.concatenate(split_table(plane), axis=0)
    source = jnp.arange(NX, dtype=jnp.int32)
    around = (source[:, None] - source[None, :] + NX // 2) % NX - NX // 2
    column = tap_weights(kernel_widths, around)
    column_high, column_low = split_table(column)
    column_table = jnp.concatenate(
        [
            jnp.concatenate([column_high, column_low], axis=2),
            jnp.concatenate([column_high, jnp.zeros_like(column_low)], axis=2),
        ],
        axis=1,
    )
    eight = jnp.eye(8, dtype=f32)
    first = (0.5 * w_in.T)[None, :, :, None] * eight[:, None, None, :]
    first_high, first_low = split_table(first.reshape(8 * HID, CHAN * 8))
    bias_high, bias_low = split_table(jnp.tile(0.5 * b_in, 8)[:, None])
    first_table = jnp.concatenate(
        [
            first_high,
            first_high,
            first_low,
            bias_high,
            bias_low,
            jnp.zeros((8 * HID, 14), bf16),
        ],
        axis=1,
    )
    two = jnp.eye(2, dtype=f32)
    middle = (two[:, None, :, None] * (0.5 * w_mid.T)[None, :, None, :]).reshape(2 * HID, 2 * HID)
    middle_high, middle_low = split_table(middle)
    middle_table = jnp.concatenate(
        [
            jnp.concatenate([middle_high, middle_high], axis=1),
            jnp.concatenate([middle_low, jnp.zeros_like(middle_low)], axis=1),
        ],
        axis=0,
    )
    middle_bias = jnp.broadcast_to(jnp.tile(0.5 * b_mid, 2)[:, None], (2 * HID, 2 * NX))
    last_weight = jnp.broadcast_to(jnp.tile(w_out, 2)[:, None], (2 * HID, 2 * NX))
    return (
        plane_table,
        column_table,
        first_table,
        middle_table,
        middle_bias,
        last_weight,
        b_out,
    )


def widen_body(position, far, near, partner, own, wide, first_planes, last_planes):
    orb = position[0]
    wide[pl.ds(HALF + HALF * orb, HALF)] = own[...]
    wide[pl.ds(2 * HALF - HALF * orb, HALF)] = partner[...]
    wide[pl.ds(3 * HALF * orb, HALF)] = near[...]
    wide[pl.ds(3 * HALF - 3 * HALF * orb, HALF)] = far[...]
    first_planes[...] = wide[:, :16, :]
    last_planes[...] = wide[...].astype(f32)[:, CZ - 16 :, :].astype(bf16)


def widen(position, far, near, partner, own):
    return pl.pallas_call(
        widen_body,
        name="widen_rows",
        out_shape=(
            jax.ShapeDtypeStruct((CY + BOX, CZ, NX), bf16),
            jax.ShapeDtypeStruct((CY + BOX, 16, NX), bf16),
            jax.ShapeDtypeStruct((CY + BOX, 16, NX), bf16),
        ),
        in_specs=[SMEM] + [VMEM] * 4,
        out_specs=(VMEM,) * 3,
        compiler_params=ROOM,
    )(position, far, near, partner, own)


def cut_body(rows, wide, below, above, windows, reach, cuts, offsets, offsets_sem, sems):
    fetch = pltpu.make_async_copy(rows, offsets, offsets_sem)
    fetch.start()
    reach[:, :16, :] = below[...].astype(f32)
    reach[:, 16 : 16 + CZ, :] = wide[...].astype(f32)
    reach[:, 16 + CZ :, :] = above[...].astype(f32)
    fetch.wait()
    lane = lanes(BOX)

    def source_step(source, carry):
        mains, tails = [], []
        for slot in range(CAP):
            z0 = offsets[source, 64 * slot] + 16 - FIRST_PLANE
            y0 = offsets[source, 64 * slot + 1]
            x0 = offsets[source, 64 * slot + 2]
            tiles = [None] * 5
            for b in range(BOX):
                tile, left = divmod(BOX * b, NX)
                piece = reach[y0 + b, pl.ds(z0, BOX), :]
                piece = pltpu.roll(piece, (left - x0) & (NX - 1), 1)
                if tiles[tile] is None:
                    tiles[tile] = piece
                else:
                    tiles[tile] = jnp.where(lane >= left, piece, tiles[tile])
                if left + BOX > NX:
                    tiles[tile + 1] = piece
            mains += tiles[:4]
            tails.append(tiles[4])
        tail = jnp.where(lane < 64, tails[0], pltpu.roll(tails[1], 64, 1))
        cuts[source] = jnp.concatenate(mains + [tail], axis=0).astype(bf16)
        return carry

    copies = []
    for first in range(0, SLABS, PART):
        lax.fori_loop(first, first + PART, source_step, 0, unroll=2)
        copy = pltpu.make_async_copy(
            cuts.at[pl.ds(first, PART)], windows.at[pl.ds(first, PART)], sems.at[first // PART]
        )
        copy.start()
        copies.append(copy)
    for copy in copies:
        copy.wait()


def cut(offsets, wide, below, above):
    return pl.pallas_call(
        cut_body,
        name="cut_windows",
        out_shape=jax.ShapeDtypeStruct((SLABS, WINDOW_ROWS, NX), bf16),
        in_specs=[VMEM] * 4,
        out_specs=pl.BlockSpec(memory_space=pl.ANY),
        scratch_shapes=[
            pltpu.VMEM((CY + BOX, CZ + 32, NX), f32),
            pltpu.VMEM((SLABS, WINDOW_ROWS, NX), bf16),
            pltpu.SMEM((SLABS, NX), jnp.int32),
            pltpu.SemaphoreType.DMA,
            pltpu.SemaphoreType.DMA((SLABS // PART,)),
        ],
        compiler_params=ROOM,
    )(offsets, wide, below, above)


def apply_body(corners, windows, orbitals, applied, count):
    def clear(slab, carry):
        count[slab] = 0
        return carry

    lax.fori_loop(0, SLABS, clear, 0)

    def place(i, carry):
        slab = lax.div(corners[0, i], CZ)
        rank = count[slab]
        count[slab] = rank + 1
        main = windows[slab, pl.ds(pl.multiple_of(rank * MAIN, 32), MAIN), :].astype(f32)
        tail = windows[slab, TAIL:WINDOW_ROWS, :].astype(f32)
        tail = jnp.where(rank == 0, tail[:, :64], tail[:, 64:])
        whole = jnp.concatenate([main[BOX * j : BOX * j + BOX] for j in range(4)] + [tail], axis=1)
        applied[i] = (whole * orbitals[i].astype(f32)).astype(bf16)
        return carry

    lax.fori_loop(0, HELD, place, 0, unroll=4)


def apply(corners, windows, orbitals):
    return pl.pallas_call(
        apply_body,
        name="apply_windows",
        out_shape=jax.ShapeDtypeStruct(orbitals.shape, bf16),
        in_specs=[SMEM, VMEM, VMEM],
        out_specs=VMEM,
        scratch_shapes=[pltpu.SMEM((SLABS,), jnp.int32)],
        compiler_params=ROOM,
    )(corners, windows, orbitals)


def exchange(x, axis):
    return lax.all_to_all(x, axis, split_axis=0, concat_axis=0, tiled=True)


def local(orbitals, occupation, corners, kernel_widths, w_in, b_in, w_mid, b_mid, w_out, b_out):
    corners = corners.T
    taps = tap_weights(kernel_widths, jnp.arange(-RAD, RAD + 1))
    tables = model_tables(kernel_widths, w_in, b_in, w_mid, b_mid, w_out, b_out)
    received = exchange(pack(corners, occupation, orbitals), "gz")
    received, taps, tables = lax.optimization_barrier((received, taps, tables))
    position = lax.axis_index("orb").reshape(1)
    own, next_up, next_down, offsets = deposit(received)
    kept, next_right, next_left = fold_planes(
        own, shifted(next_up, "gz", 1), shifted(next_down, "gz", -1)
    )
    left = across_rows(next_right, (1, 1), 1)
    right = across_rows(next_left, (-1, -1), 1)
    kept, given = fold_rows(position, kept, left, right)
    half = model(kept, shifted(given, "orb", 1), taps, tables)
    far = across_rows(half, (-1, 1), 0)
    near = across_rows(half, (-1, 1), 1)
    partner = shifted(half, "orb", 1)
    wide, first_planes, last_planes = widen(position, far, near, partner, half)
    below = shifted(last_planes, "gz", 1)
    above = shifted(first_planes, "gz", -1)
    windows = cut(offsets, wide, below, above)
    applied = apply(corners, exchange(windows, "gz"), orbitals)
    tile = jnp.concatenate([below[:CY, 16 - FIRST_PLANE :], wide[:CY, : CZ - FIRST_PLANE]], axis=1)
    return jnp.transpose(tile, (1, 0, 2)), applied


def solution(mesh):
    return jax.shard_map(
        local,
        mesh=mesh,
        in_specs=(
            P(("gz", "gy", "orb"), None, None),
            P(("gz", "gy", "orb")),
            P(("gz", "gy", "orb"), None),
            P(),
            P(),
            P(),
            P(),
            P(),
            P(),
            P(),
        ),
        out_specs=(P("gz", "gy", None), P(("gz", "gy", "orb"), None, None)),
        check_vma=False,
    )
```

```python
import jax
import jax.numpy as jnp
from jax import lax
from jax.experimental import pallas as pl
from jax.experimental.pallas import tpu as pltpu
from jax.sharding import PartitionSpec as P

BOX = 24
CHAN = 8
HID = 64
RAD = 6
CZ = 24
CY = 24
NX = 128
CAP = 2
SLABS = 16
HELD = 16
FIRST_PLANE = 10
PLANES = 40
ABOVE = PLANES - CZ
HALF = CY // 2
ROWS = HALF + 2 * RAD
REACH = CY + 2 * RAD
EDGE = REACH // 2
MAIN = 96
TAIL = CAP * MAIN
BLOCK_ROWS = 224
GROUP = 4
PART = 4
WINDOW_ROWS = TAIL + BOX

VMEM = pl.BlockSpec(memory_space=pltpu.VMEM)
SMEM = pl.BlockSpec(memory_space=pltpu.SMEM)
ROOM = pltpu.CompilerParams(vmem_limit_bytes=16 * 1024 * 1024)
f32 = jnp.float32
bf16 = jnp.bfloat16


def shifted(x, axis, by):
    count = lax.axis_size(axis)
    return lax.ppermute(x, axis, [(i, (i + by) % count) for i in range(count)])


def across_rows(x, steps, cross):
    tiles, owners = lax.axis_size("gy"), lax.axis_size("orb")
    pairs = [
        (tile * owners + orb, (tile + steps[orb]) % tiles * owners + (orb + cross) % owners)
        for tile in range(tiles)
        for orb in range(owners)
    ]
    return lax.ppermute(x, ("gy", "orb"), pairs)


def split(x):
    high = x.astype(bf16)
    return high, (x - high.astype(f32)).astype(bf16)


def split_table(x):
    high = lax.reduce_precision(x, 8, 7)
    return high.astype(bf16), (x - high).astype(bf16)


def lanes(rows):
    return lax.broadcasted_iota(jnp.int32, (rows, NX), 1)


def pack_body(corners_in, occupation_in, orbitals, sent, boxes, corners, occupation, count, scalar_sems, sems):
    scalars = [
        pltpu.make_async_copy(corners_in, corners, scalar_sems.at[0]),
        pltpu.make_async_copy(occupation_in, occupation, scalar_sems.at[1]),
    ]
    for copy in scalars:
        copy.start()
    copies = [
        pltpu.make_async_copy(
            orbitals.at[pl.ds(PART * i, PART)], boxes.at[pl.ds(PART * i, PART)], sems.at[i]
        )
        for i in range(HELD // PART)
    ]
    for copy in copies:
        copy.start()
    sent[...] = jnp.zeros(sent.shape, bf16)

    def clear(slab, carry):
        count[slab] = 0
        return carry

    lax.fori_loop(0, SLABS, clear, 0)
    side = lanes(32) // 64
    field = lanes(8) % 64

    def place(i):
        plane = corners[0, i]
        row = corners[1, i]
        column = corners[2, i]
        slab = lax.div(plane, CZ)
        rank = count[slab]
        count[slab] = rank + 1
        values = boxes[i].astype(f32)
        density = occupation[i] * values * values
        main = jnp.concatenate([density[:, 128 * j : 128 * j + 128] for j in range(4)], axis=0)
        sent[slab, pl.ds(pl.multiple_of(rank * MAIN, 32), MAIN), :] = main.astype(bf16)
        last = density[:, 512:576]
        tail = jnp.concatenate([last, last], axis=1)
        offsets = jnp.where(
            field == 0,
            lax.rem(plane, CZ),
            jnp.where(field == 1, lax.rem(row, CY), jnp.where(field == 2, column, 0)),
        ).astype(f32)
        fresh = jnp.concatenate([tail, offsets], axis=0)
        held = sent[slab, TAIL:BLOCK_ROWS, :].astype(f32)
        sent[slab, TAIL:BLOCK_ROWS, :] = jnp.where(side == rank, fresh, held).astype(bf16)

    for copy in scalars:
        copy.wait()
    for i in range(HELD):
        if i % PART == 0:
            copies[i // PART].wait()
        place(i)


def pack(corners, occupation, orbitals):
    return pl.pallas_call(
        pack_body,
        name="pack_boxes",
        out_shape=jax.ShapeDtypeStruct((SLABS, BLOCK_ROWS, NX), bf16),
        in_specs=[pl.BlockSpec(memory_space=pl.ANY)] * 3,
        out_specs=VMEM,
        scratch_shapes=[
            pltpu.VMEM((HELD, BOX, BOX * BOX), bf16),
            pltpu.SMEM((3, HELD), jnp.int32),
            pltpu.SMEM((HELD,), f32),
            pltpu.SMEM((SLABS,), jnp.int32),
            pltpu.SemaphoreType.DMA((2,)),
            pltpu.SemaphoreType.DMA((HELD // PART,)),
        ],
        compiler_params=pltpu.CompilerParams(vmem_limit_bytes=60 * 1024 * 1024),
    )(corners, occupation, orbitals)


def read_offsets(received, rows, offsets, sem):
    for source in range(SLABS):
        rows[source : source + 1, :] = (
            received[source, 208:BLOCK_ROWS, :].astype(f32)[8:9].astype(jnp.int32)
        )
    copy = pltpu.make_async_copy(rows, offsets, sem)
    copy.start()
    return copy


def deposit_body(received, own, next_up, next_down, offsets_out, grids, rows, offsets, sem):
    copy = read_offsets(received, rows, offsets, sem)
    offsets_out[...] = rows[...]
    for grid in grids:
        grid[...] = jnp.zeros(grid.shape, f32)
    copy.wait()
    lane = lanes(BOX)

    def source_step(source, carry):
        tail_both = received[source, TAIL:BLOCK_ROWS, :].astype(f32)[:BOX]
        boxes = []
        for slot in range(CAP):
            start = [offsets[source, 64 * slot + field] for field in range(3)]
            main = received[source, MAIN * slot : MAIN * slot + MAIN, :].astype(f32)
            tiles = [main[BOX * j : BOX * j + BOX] for j in range(4)]
            tiles.append(tail_both if slot == 0 else pltpu.roll(tail_both, 64, 1))
            boxes.append((start, tiles, ((lane - start[2]) & (NX - 1)) < BOX))
        for first in range(0, BOX, GROUP):
            for slot in range(CAP):
                (z0, y0, x0), tiles, inside = boxes[slot]
                grid = grids[slot]
                olds = [grid[y0 + first + k, pl.ds(z0, BOX), :] for k in range(GROUP)]
                news = []
                for k in range(GROUP):
                    tile, left = divmod(BOX * (first + k), NX)
                    piece = tiles[tile]
                    if left + BOX > NX:
                        piece = jnp.where(lane >= left, piece, tiles[tile + 1])
                    piece = pltpu.roll(piece, (x0 - left) & (NX - 1), 1)
                    news.append(olds[k] + jnp.where(inside, piece, 0.0))
                for k in range(GROUP):
                    grid[y0 + first + k, pl.ds(z0, BOX), :] = news[k]
        return carry

    lax.fori_loop(0, SLABS, source_step, 0, unroll=2)
    own[...] = grids[0][:, :PLANES, :] + grids[1][:, :PLANES, :]
    next_up[...] = (grids[0][:, CZ:, :] + grids[1][:, CZ:, :]).astype(bf16)
    next_down[...] = (grids[0][:, :ABOVE, :] + grids[1][:, :ABOVE, :]).astype(bf16)


def deposit(received):
    return pl.pallas_call(
        deposit_body,
        name="deposit_boxes",
        out_shape=(
            jax.ShapeDtypeStruct((CY + BOX, PLANES, NX), f32),
            jax.ShapeDtypeStruct((CY + BOX, BOX, NX), bf16),
            jax.ShapeDtypeStruct((CY + BOX, ABOVE, NX), bf16),
            jax.ShapeDtypeStruct((SLABS, NX), jnp.int32),
        ),
        in_specs=[VMEM],
        out_specs=(VMEM,) * 4,
        scratch_shapes=[
            [pltpu.VMEM((CY + BOX, CZ + BOX, NX), f32)] * CAP,
            pltpu.VMEM((SLABS, NX), jnp.int32),
            pltpu.SMEM((SLABS, NX), jnp.int32),
            pltpu.SemaphoreType.DMA,
        ],
        compiler_params=ROOM,
    )(received)


def fold_planes_body(own, below, above, kept, next_right, next_left):
    for first, last in ((0, CZ), (CZ, PLANES)):
        other = below[...] if first == 0 else above[...]
        total = own[:, first:last, :] + other.astype(f32)
        kept[:, first:last, :] = total[RAD : RAD + REACH]
        next_right[:, first:last, :] = total[2 * CY - EDGE :].astype(bf16)
        next_left[:, first:last, :] = total[:EDGE].astype(bf16)


def fold_planes(own, below, above):
    return pl.pallas_call(
        fold_planes_body,
        name="fold_planes",
        out_shape=(
            jax.ShapeDtypeStruct((REACH, PLANES, NX), f32),
            jax.ShapeDtypeStruct((EDGE, PLANES, NX), bf16),
            jax.ShapeDtypeStruct((EDGE, PLANES, NX), bf16),
        ),
        in_specs=[VMEM] * 3,
        out_specs=(VMEM,) * 3,
        compiler_params=ROOM,
    )(own, below, above)


def fold_rows_body(position, own, left, right, kept, given, total):
    total[:EDGE] = own[:EDGE] + left[...].astype(f32)
    total[EDGE:] = own[EDGE:] + right[...].astype(f32)
    orb = position[0]
    kept[...] = total[pl.ds(HALF * orb, ROWS)]
    given[...] = total[pl.ds(HALF * (1 - orb), ROWS)].astype(bf16)


def fold_rows(position, own, left, right):
    return pl.pallas_call(
        fold_rows_body,
        name="fold_rows",
        out_shape=(
            jax.ShapeDtypeStruct((ROWS, PLANES, NX), f32),
            jax.ShapeDtypeStruct((ROWS, PLANES, NX), bf16),
        ),
        in_specs=[SMEM] + [VMEM] * 3,
        out_specs=(VMEM, VMEM),
        scratch_shapes=[pltpu.VMEM((REACH, PLANES, NX), f32)],
        compiler_params=ROOM,
    )(position, own, left, right)


def model_body(
    taps,
    kept,
    other,
    plane_table,
    column_table,
    first_table,
    middle_table,
    middle_bias,
    last_weight,
    last_bias,
    potential,
    planes,
    features,
    result,
):
    def plane_step(pair, carry):
        density = kept[pl.ds(2 * pair, 2)] + other[pl.ds(2 * pair, 2)].astype(f32)
        density = density.astype(bf16)
        field = jnp.concatenate([density[0], density[1]], axis=1)
        both = jnp.dot(plane_table[...], field, preferred_element_type=f32)
        total = both[: CHAN * CZ] + both[CHAN * CZ :]
        planes[2 * pair] = total[:, :NX]
        planes[2 * pair + 1] = total[:, NX:]
        return carry

    lax.fori_loop(0, ROWS // 2, plane_step, 0, unroll=12)

    def channel_step(channel, carry):
        weights = [taps[channel, step] for step in range(RAD + 1)]
        lines = []
        for part in range(CZ // 8):
            start = pl.multiple_of(channel * CZ + 8 * part, 8)
            rows = [planes[y, pl.ds(start, 8), :] for y in range(ROWS)]
            for y in range(HALF):
                total = weights[RAD] * rows[y + RAD]
                for step in range(RAD):
                    total = total + weights[step] * (rows[y + step] + rows[y + 2 * RAD - step])
                lines.append(total)
        high, low = split(jnp.concatenate(lines, axis=0))
        both = jnp.dot(
            jnp.concatenate([high, low], axis=1), column_table[channel], preferred_element_type=f32
        )
        smooth = both[:, :NX] + both[:, NX:]
        features[channel] = jnp.log(1.0 + smooth)
        return carry

    lax.fori_loop(0, CHAN, channel_step, 0, unroll=8)

    def cell_step(step, carry):
        start = pl.multiple_of(step * 16, 16)
        inputs = [features[channel, pl.ds(start, 16), :] for channel in range(CHAN)]
        cells = jnp.concatenate(
            [
                jnp.concatenate([piece[:8] for piece in inputs], axis=0),
                jnp.concatenate([piece[8:] for piece in inputs], axis=0),
            ],
            axis=1,
        )
        high, low = split(cells)
        ones = jnp.ones((16, 2 * NX), bf16)
        stacked = jnp.concatenate([high, low, high, ones], axis=0)
        values = []
        for half in range(2):
            hidden = jnp.dot(
                first_table[256 * half : 256 * half + 256, :], stacked, preferred_element_type=f32
            )
            hidden = hidden + hidden * jnp.tanh(hidden)
            hidden_high, hidden_low = split(hidden)
            for pair in range(2):
                rows = slice(128 * pair, 128 * pair + 128)
                both = jnp.dot(
                    middle_table[...],
                    jnp.concatenate([hidden_high[rows], hidden_low[rows]], axis=0),
                    preferred_element_type=f32,
                )
                mixed = both[:128] + both[128:] + middle_bias[...]
                mixed = (mixed + mixed * jnp.tanh(mixed)) * last_weight[...]
                values.append(jnp.sum(mixed.reshape(2, HID, 2 * NX), axis=1))
        value = jnp.concatenate(values, axis=0) + last_bias[0]
        result[pl.ds(start, 8), :] = value[:, :NX]
        result[pl.ds(start + 8, 8), :] = value[:, NX:]
        return carry

    lax.fori_loop(0, CZ * HALF // 16, cell_step, 0, unroll=9)
    for part in range(CZ // 8):
        block = result[HALF * 8 * part : HALF * 8 * (part + 1), :]
        planes[:HALF, 8 * part : 8 * part + 8, :] = block.reshape(HALF, 8, NX)
    potential[...] = planes[:HALF, :CZ, :].astype(bf16)


def model(kept, other, taps, tables):
    return pl.pallas_call(
        model_body,
        name="smooth_and_network",
        out_shape=jax.ShapeDtypeStruct((HALF, CZ, NX), bf16),
        in_specs=[SMEM] + [VMEM] * 8 + [SMEM],
        out_specs=VMEM,
        scratch_shapes=[
            pltpu.VMEM((ROWS, CHAN * CZ, NX), f32),
            pltpu.VMEM((CHAN, HALF * CZ, NX), f32),
            pltpu.VMEM((HALF * CZ, NX), f32),
        ],
        compiler_params=ROOM,
    )(taps, kept, other, *tables)


def tap_weights(kernel_widths, distance):
    width = kernel_widths.reshape((CHAN,) + (1,) * distance.ndim)
    reach = jnp.arange(-RAD, RAD + 1).astype(f32).reshape((2 * RAD + 1,) + (1,) * distance.ndim)
    whole = jnp.sum(jnp.exp(-(reach**2)[None] / (2.0 * width[:, None] ** 2)), axis=1)
    far = distance.astype(f32)[None]
    raw = jnp.where(jnp.abs(far) <= RAD, jnp.exp(-(far**2) / (2.0 * width**2)), 0.0)
    return raw / whole


def model_tables(kernel_widths, w_in, b_in, w_mid, b_mid, w_out, b_out):
    out_index = jnp.arange(CZ, dtype=jnp.int32)
    in_index = jnp.arange(PLANES, dtype=jnp.int32) - FIRST_PLANE
    plane = tap_weights(kernel_widths, in_index[None, :] - out_index[:, None])
    plane = plane.reshape(CHAN * CZ, PLANES)
    plane_table = jnp.concatenate(split_table(plane), axis=0)
    source = jnp.arange(NX, dtype=jnp.int32)
    around = (source[:, None] - source[None, :] + NX // 2) % NX - NX // 2
    column = tap_weights(kernel_widths, around)
    column_high, column_low = split_table(column)
    column_table = jnp.concatenate(
        [
            jnp.concatenate([column_high, column_low], axis=2),
            jnp.concatenate([column_high, jnp.zeros_like(column_low)], axis=2),
        ],
        axis=1,
    )
    eight = jnp.eye(8, dtype=f32)
    first = (0.5 * w_in.T)[None, :, :, None] * eight[:, None, None, :]
    first_high, first_low = split_table(first.reshape(8 * HID, CHAN * 8))
    bias_high, bias_low = split_table(jnp.tile(0.5 * b_in, 8)[:, None])
    first_table = jnp.concatenate(
        [
            first_high,
            first_high,
            first_low,
            bias_high,
            bias_low,
            jnp.zeros((8 * HID, 14), bf16),
        ],
        axis=1,
    )
    two = jnp.eye(2, dtype=f32)
    middle = (two[:, None, :, None] * (0.5 * w_mid.T)[None, :, None, :]).reshape(2 * HID, 2 * HID)
    middle_high, middle_low = split_table(middle)
    middle_table = jnp.concatenate(
        [
            jnp.concatenate([middle_high, middle_high], axis=1),
            jnp.concatenate([middle_low, jnp.zeros_like(middle_low)], axis=1),
        ],
        axis=0,
    )
    middle_bias = jnp.broadcast_to(jnp.tile(0.5 * b_mid, 2)[:, None], (2 * HID, 2 * NX))
    last_weight = jnp.broadcast_to(jnp.tile(w_out, 2)[:, None], (2 * HID, 2 * NX))
    return (
        plane_table,
        column_table,
        first_table,
        middle_table,
        middle_bias,
        last_weight,
        b_out,
    )


def widen_body(position, far, near, partner, own, wide, first_planes, last_planes):
    orb = position[0]
    wide[pl.ds(HALF + HALF * orb, HALF)] = own[...]
    wide[pl.ds(2 * HALF - HALF * orb, HALF)] = partner[...]
    wide[pl.ds(3 * HALF * orb, HALF)] = near[...]
    wide[pl.ds(3 * HALF - 3 * HALF * orb, HALF)] = far[...]
    first_planes[...] = wide[:, :16, :]
    last_planes[...] = wide[...].astype(f32)[:, CZ - 16 :, :].astype(bf16)


def widen(position, far, near, partner, own):
    return pl.pallas_call(
        widen_body,
        name="widen_rows",
        out_shape=(
            jax.ShapeDtypeStruct((CY + BOX, CZ, NX), bf16),
            jax.ShapeDtypeStruct((CY + BOX, 16, NX), bf16),
            jax.ShapeDtypeStruct((CY + BOX, 16, NX), bf16),
        ),
        in_specs=[SMEM] + [VMEM] * 4,
        out_specs=(VMEM,) * 3,
        compiler_params=ROOM,
    )(position, far, near, partner, own)


def cut_body(rows, wide, below, above, windows, reach, cuts, offsets, offsets_sem, sems):
    fetch = pltpu.make_async_copy(rows, offsets, offsets_sem)
    fetch.start()
    reach[:, :16, :] = below[...].astype(f32)
    reach[:, 16 : 16 + CZ, :] = wide[...].astype(f32)
    reach[:, 16 + CZ :, :] = above[...].astype(f32)
    fetch.wait()
    lane = lanes(BOX)

    def source_step(source, carry):
        mains, tails = [], []
        for slot in range(CAP):
            z0 = offsets[source, 64 * slot] + 16 - FIRST_PLANE
            y0 = offsets[source, 64 * slot + 1]
            x0 = offsets[source, 64 * slot + 2]
            tiles = [None] * 5
            for b in range(BOX):
                tile, left = divmod(BOX * b, NX)
                piece = reach[y0 + b, pl.ds(z0, BOX), :]
                piece = pltpu.roll(piece, (left - x0) & (NX - 1), 1)
                if tiles[tile] is None:
                    tiles[tile] = piece
                else:
                    tiles[tile] = jnp.where(lane >= left, piece, tiles[tile])
                if left + BOX > NX:
                    tiles[tile + 1] = piece
            mains += tiles[:4]
            tails.append(tiles[4])
        tail = jnp.where(lane < 64, tails[0], pltpu.roll(tails[1], 64, 1))
        cuts[source] = jnp.concatenate(mains + [tail], axis=0).astype(bf16)
        return carry

    copies = []
    for first in range(0, SLABS, PART):
        lax.fori_loop(first, first + PART, source_step, 0, unroll=4)
        copy = pltpu.make_async_copy(
            cuts.at[pl.ds(first, PART)], windows.at[pl.ds(first, PART)], sems.at[first // PART]
        )
        copy.start()
        copies.append(copy)
    for copy in copies:
        copy.wait()


def cut(offsets, wide, below, above):
    return pl.pallas_call(
        cut_body,
        name="cut_windows",
        out_shape=jax.ShapeDtypeStruct((SLABS, WINDOW_ROWS, NX), bf16),
        in_specs=[VMEM] * 4,
        out_specs=pl.BlockSpec(memory_space=pl.ANY),
        scratch_shapes=[
            pltpu.VMEM((CY + BOX, CZ + 32, NX), f32),
            pltpu.VMEM((SLABS, WINDOW_ROWS, NX), bf16),
            pltpu.SMEM((SLABS, NX), jnp.int32),
            pltpu.SemaphoreType.DMA,
            pltpu.SemaphoreType.DMA((SLABS // PART,)),
        ],
        compiler_params=ROOM,
    )(offsets, wide, below, above)


def apply_body(corners, windows, orbitals, applied, products, count, sems):
    def clear(slab, carry):
        count[slab] = 0
        return carry

    lax.fori_loop(0, SLABS, clear, 0)

    def place(i, carry):
        slab = lax.div(corners[0, i], CZ)
        rank = count[slab]
        count[slab] = rank + 1
        main = windows[slab, pl.ds(pl.multiple_of(rank * MAIN, 32), MAIN), :].astype(f32)
        tail = windows[slab, TAIL:WINDOW_ROWS, :].astype(f32)
        tail = jnp.where(rank == 0, tail[:, :64], tail[:, 64:])
        whole = jnp.concatenate([main[BOX * j : BOX * j + BOX] for j in range(4)] + [tail], axis=1)
        products[i] = (whole * orbitals[i].astype(f32)).astype(bf16)
        return carry

    copies = []
    for first in range(0, HELD, PART):
        lax.fori_loop(first, first + PART, place, 0, unroll=4)
        copy = pltpu.make_async_copy(
            products.at[pl.ds(first, PART)], applied.at[pl.ds(first, PART)], sems.at[first // PART]
        )
        copy.start()
        copies.append(copy)
    for copy in copies:
        copy.wait()


def apply(corners, windows, orbitals):
    return pl.pallas_call(
        apply_body,
        name="apply_windows",
        out_shape=jax.ShapeDtypeStruct(orbitals.shape, bf16),
        in_specs=[SMEM, VMEM, VMEM],
        out_specs=pl.BlockSpec(memory_space=pl.ANY),
        scratch_shapes=[
            pltpu.VMEM((HELD, BOX, BOX * BOX), bf16),
            pltpu.SMEM((SLABS,), jnp.int32),
            pltpu.SemaphoreType.DMA((HELD // PART,)),
        ],
        compiler_params=ROOM,
    )(corners, windows, orbitals)


def exchange(x, axis):
    return lax.all_to_all(x, axis, split_axis=0, concat_axis=0, tiled=True)


def local(orbitals, occupation, corners, kernel_widths, w_in, b_in, w_mid, b_mid, w_out, b_out):
    corners = corners.T
    taps = tap_weights(kernel_widths, jnp.arange(-RAD, RAD + 1))
    tables = model_tables(kernel_widths, w_in, b_in, w_mid, b_mid, w_out, b_out)
    received = exchange(pack(corners, occupation, orbitals), "gz")
    received, taps, tables = lax.optimization_barrier((received, taps, tables))
    position = lax.axis_index("orb").reshape(1)
    own, next_up, next_down, offsets = deposit(received)
    kept, next_right, next_left = fold_planes(
        own, shifted(next_up, "gz", 1), shifted(next_down, "gz", -1)
    )
    left = across_rows(next_right, (1, 1), 1)
    right = across_rows(next_left, (-1, -1), 1)
    kept, given = fold_rows(position, kept, left, right)
    half = model(kept, shifted(given, "orb", 1), taps, tables)
    far = across_rows(half, (-1, 1), 0)
    near = across_rows(half, (-1, 1), 1)
    partner = shifted(half, "orb", 1)
    wide, first_planes, last_planes = widen(position, far, near, partner, half)
    below = shifted(last_planes, "gz", 1)
    above = shifted(first_planes, "gz", -1)
    windows = cut(offsets, wide, below, above)
    applied = apply(corners, exchange(windows, "gz"), orbitals)
    tile = jnp.concatenate([below[:CY, 16 - FIRST_PLANE :], wide[:CY, : CZ - FIRST_PLANE]], axis=1)
    return jnp.transpose(tile, (1, 0, 2)), applied


def solution(mesh):
    return jax.shard_map(
        local,
        mesh=mesh,
        in_specs=(
            P(("gz", "gy", "orb"), None, None),
            P(("gz", "gy", "orb")),
            P(("gz", "gy", "orb"), None),
            P(),
            P(),
            P(),
            P(),
            P(),
            P(),
            P(),
        ),
        out_specs=(P("gz", "gy", None), P(("gz", "gy", "orb"), None, None)),
        check_vma=False,
    )
```

```python
import jax
import jax.numpy as jnp
from jax import lax
from jax.experimental import pallas as pl
from jax.experimental.pallas import tpu as pltpu
from jax.sharding import PartitionSpec as P

BOX = 24
CHAN = 8
HID = 64
RAD = 6
CZ = 24
CY = 24
NX = 128
CAP = 2
SLABS = 16
HELD = 16
FIRST_PLANE = 10
PLANES = 40
SKIP = FIRST_PLANE - RAD
DEPTH = PLANES - SKIP
ABOVE = PLANES - CZ
HALF = CY // 2
ROWS = HALF + 2 * RAD
REACH = CY + 2 * RAD
EDGE = REACH // 2
MAIN = 96
TAIL = CAP * MAIN
BLOCK_ROWS = 224
GROUP = 4
PART = 4
WINDOW_ROWS = TAIL + BOX

VMEM = pl.BlockSpec(memory_space=pltpu.VMEM)
SMEM = pl.BlockSpec(memory_space=pltpu.SMEM)
ROOM = pltpu.CompilerParams(vmem_limit_bytes=16 * 1024 * 1024)
f32 = jnp.float32
bf16 = jnp.bfloat16


def shifted(x, axis, by):
    count = lax.axis_size(axis)
    return lax.ppermute(x, axis, [(i, (i + by) % count) for i in range(count)])


def across_rows(x, steps, cross):
    tiles, owners = lax.axis_size("gy"), lax.axis_size("orb")
    pairs = [
        (tile * owners + orb, (tile + steps[orb]) % tiles * owners + (orb + cross) % owners)
        for tile in range(tiles)
        for orb in range(owners)
    ]
    return lax.ppermute(x, ("gy", "orb"), pairs)


def split(x):
    high = x.astype(bf16)
    return high, (x - high.astype(f32)).astype(bf16)


def split_table(x):
    high = lax.reduce_precision(x, 8, 7)
    return high.astype(bf16), (x - high).astype(bf16)


def lanes(rows):
    return lax.broadcasted_iota(jnp.int32, (rows, NX), 1)


def pack_body(corners_in, occupation_in, orbitals, sent, boxes, corners, occupation, count, scalar_sems, sems):
    scalars = [
        pltpu.make_async_copy(corners_in, corners, scalar_sems.at[0]),
        pltpu.make_async_copy(occupation_in, occupation, scalar_sems.at[1]),
    ]
    for copy in scalars:
        copy.start()
    copies = [
        pltpu.make_async_copy(
            orbitals.at[pl.ds(PART * i, PART)], boxes.at[pl.ds(PART * i, PART)], sems.at[i]
        )
        for i in range(HELD // PART)
    ]
    for copy in copies:
        copy.start()
    sent[...] = jnp.zeros(sent.shape, bf16)

    def clear(slab, carry):
        count[slab] = 0
        return carry

    lax.fori_loop(0, SLABS, clear, 0)
    side = lanes(32) // 64
    field = lanes(8) % 64

    def place(i):
        plane = corners[0, i]
        row = corners[1, i]
        column = corners[2, i]
        slab = lax.div(plane, CZ)
        rank = count[slab]
        count[slab] = rank + 1
        values = boxes[i].astype(f32)
        density = occupation[i] * values * values
        main = jnp.concatenate([density[:, 128 * j : 128 * j + 128] for j in range(4)], axis=0)
        sent[slab, pl.ds(pl.multiple_of(rank * MAIN, 32), MAIN), :] = main.astype(bf16)
        last = density[:, 512:576]
        tail = jnp.concatenate([last, last], axis=1)
        offsets = jnp.where(
            field == 0,
            lax.rem(plane, CZ),
            jnp.where(field == 1, lax.rem(row, CY), jnp.where(field == 2, column, 0)),
        ).astype(f32)
        fresh = jnp.concatenate([tail, offsets], axis=0)
        held = sent[slab, TAIL:BLOCK_ROWS, :].astype(f32)
        sent[slab, TAIL:BLOCK_ROWS, :] = jnp.where(side == rank, fresh, held).astype(bf16)

    for copy in scalars:
        copy.wait()
    for i in range(HELD):
        if i % PART == 0:
            copies[i // PART].wait()
        place(i)


def pack(corners, occupation, orbitals):
    return pl.pallas_call(
        pack_body,
        name="pack_boxes",
        out_shape=jax.ShapeDtypeStruct((SLABS, BLOCK_ROWS, NX), bf16),
        in_specs=[pl.BlockSpec(memory_space=pl.ANY)] * 3,
        out_specs=VMEM,
        scratch_shapes=[
            pltpu.VMEM((HELD, BOX, BOX * BOX), bf16),
            pltpu.SMEM((3, HELD), jnp.int32),
            pltpu.SMEM((HELD,), f32),
            pltpu.SMEM((SLABS,), jnp.int32),
            pltpu.SemaphoreType.DMA((2,)),
            pltpu.SemaphoreType.DMA((HELD // PART,)),
        ],
        compiler_params=pltpu.CompilerParams(vmem_limit_bytes=60 * 1024 * 1024),
    )(corners, occupation, orbitals)


def read_offsets(received, rows, offsets, sem):
    for source in range(SLABS):
        rows[source : source + 1, :] = (
            received[source, 208:BLOCK_ROWS, :].astype(f32)[8:9].astype(jnp.int32)
        )
    copy = pltpu.make_async_copy(rows, offsets, sem)
    copy.start()
    return copy


def deposit_body(received, own, next_up, next_down, offsets_out, grids, rows, offsets, sem):
    copy = read_offsets(received, rows, offsets, sem)
    offsets_out[...] = rows[...]
    for grid in grids:
        grid[...] = jnp.zeros(grid.shape, f32)
    copy.wait()
    lane = lanes(BOX)

    def source_step(source, carry):
        tail_both = received[source, TAIL:BLOCK_ROWS, :].astype(f32)[:BOX]
        boxes = []
        for slot in range(CAP):
            start = [offsets[source, 64 * slot + field] for field in range(3)]
            main = received[source, MAIN * slot : MAIN * slot + MAIN, :].astype(f32)
            tiles = [main[BOX * j : BOX * j + BOX] for j in range(4)]
            tiles.append(tail_both if slot == 0 else pltpu.roll(tail_both, 64, 1))
            boxes.append((start, tiles, ((lane - start[2]) & (NX - 1)) < BOX))
        for first in range(0, BOX, GROUP):
            for slot in range(CAP):
                (z0, y0, x0), tiles, inside = boxes[slot]
                grid = grids[slot]
                olds = [grid[y0 + first + k, pl.ds(z0, BOX), :] for k in range(GROUP)]
                news = []
                for k in range(GROUP):
                    tile, left = divmod(BOX * (first + k), NX)
                    piece = tiles[tile]
                    if left + BOX > NX:
                        piece = jnp.where(lane >= left, piece, tiles[tile + 1])
                    piece = pltpu.roll(piece, (x0 - left) & (NX - 1), 1)
                    news.append(olds[k] + jnp.where(inside, piece, 0.0))
                for k in range(GROUP):
                    grid[y0 + first + k, pl.ds(z0, BOX), :] = news[k]
        return carry

    lax.fori_loop(0, SLABS, source_step, 0, unroll=2)
    own[...] = grids[0][:, :PLANES, :] + grids[1][:, :PLANES, :]
    next_up[...] = (grids[0][:, CZ:, :] + grids[1][:, CZ:, :]).astype(bf16)
    next_down[...] = (grids[0][:, :ABOVE, :] + grids[1][:, :ABOVE, :]).astype(bf16)


def deposit(received):
    return pl.pallas_call(
        deposit_body,
        name="deposit_boxes",
        out_shape=(
            jax.ShapeDtypeStruct((CY + BOX, PLANES, NX), f32),
            jax.ShapeDtypeStruct((CY + BOX, BOX, NX), bf16),
            jax.ShapeDtypeStruct((CY + BOX, ABOVE, NX), bf16),
            jax.ShapeDtypeStruct((SLABS, NX), jnp.int32),
        ),
        in_specs=[VMEM],
        out_specs=(VMEM,) * 4,
        scratch_shapes=[
            [pltpu.VMEM((CY + BOX, CZ + BOX, NX), f32)] * CAP,
            pltpu.VMEM((SLABS, NX), jnp.int32),
            pltpu.SMEM((SLABS, NX), jnp.int32),
            pltpu.SemaphoreType.DMA,
        ],
        compiler_params=ROOM,
    )(received)


def fold_planes_body(own, below, above, kept, next_right, next_left, total, flat):
    total[:, :CZ, :] = own[:, :CZ, :] + below[...].astype(f32)
    total[:, CZ:, :] = own[:, CZ:, :] + above[...].astype(f32)
    kept[...] = total[RAD : RAD + REACH, SKIP:, :]
    for side, first, sent in ((0, 2 * CY - EDGE, next_right), (1, 0, next_left)):
        for row in range(EDGE):
            flat[side, DEPTH * row : DEPTH * (row + 1), :] = total[first + row, SKIP:, :]
        sent[...] = flat[side].astype(bf16)


def fold_planes(own, below, above):
    return pl.pallas_call(
        fold_planes_body,
        name="fold_planes",
        out_shape=(
            jax.ShapeDtypeStruct((REACH, DEPTH, NX), f32),
            jax.ShapeDtypeStruct((EDGE * DEPTH, NX), bf16),
            jax.ShapeDtypeStruct((EDGE * DEPTH, NX), bf16),
        ),
        in_specs=[VMEM] * 3,
        out_specs=(VMEM,) * 3,
        scratch_shapes=[
            pltpu.VMEM((CY + BOX, PLANES, NX), f32),
            pltpu.VMEM((2, EDGE * DEPTH, NX), f32),
        ],
        compiler_params=ROOM,
    )(own, below, above)


def fold_rows_body(position, own, left, right, kept, given, total, sides, flat):
    for side, received in enumerate((left, right)):
        sides[side] = received[...].astype(f32)
        for row in range(EDGE):
            total[EDGE * side + row] = (
                own[EDGE * side + row] + sides[side, DEPTH * row : DEPTH * (row + 1), :]
            )
    orb = position[0]
    kept[...] = total[pl.ds(HALF * orb, ROWS)]
    for row in range(ROWS):
        flat[DEPTH * row : DEPTH * (row + 1), :] = total[HALF * (1 - orb) + row]
    given[...] = flat[...].astype(bf16)


def fold_rows(position, own, left, right):
    return pl.pallas_call(
        fold_rows_body,
        name="fold_rows",
        out_shape=(
            jax.ShapeDtypeStruct((ROWS, DEPTH, NX), f32),
            jax.ShapeDtypeStruct((ROWS * DEPTH, NX), bf16),
        ),
        in_specs=[SMEM] + [VMEM] * 3,
        out_specs=(VMEM, VMEM),
        scratch_shapes=[
            pltpu.VMEM((REACH, DEPTH, NX), f32),
            pltpu.VMEM((2, EDGE * DEPTH, NX), f32),
            pltpu.VMEM((ROWS * DEPTH, NX), f32),
        ],
        compiler_params=ROOM,
    )(position, own, left, right)


def model_body(
    taps,
    kept,
    other,
    plane_table,
    column_table,
    first_table,
    middle_table,
    middle_bias,
    last_weight,
    last_bias,
    potential,
    planes,
    features,
    result,
    flat,
):
    flat[...] = other[...].astype(f32)

    def plane_step(pair, carry):
        density = [
            kept[row] + flat[pl.ds(DEPTH * row, DEPTH), :] for row in (2 * pair, 2 * pair + 1)
        ]
        field = jnp.concatenate(density, axis=1).astype(bf16)
        both = jnp.dot(plane_table[...], field, preferred_element_type=f32)
        total = both[: CHAN * CZ] + both[CHAN * CZ :]
        planes[2 * pair] = total[:, :NX]
        planes[2 * pair + 1] = total[:, NX:]
        return carry

    lax.fori_loop(0, ROWS // 2, plane_step, 0, unroll=12)

    def channel_step(channel, carry):
        weights = [taps[channel, step] for step in range(RAD + 1)]
        lines = []
        for part in range(CZ // 8):
            start = pl.multiple_of(channel * CZ + 8 * part, 8)
            rows = [planes[y, pl.ds(start, 8), :] for y in range(ROWS)]
            for y in range(HALF):
                total = weights[RAD] * rows[y + RAD]
                for step in range(RAD):
                    total = total + weights[step] * (rows[y + step] + rows[y + 2 * RAD - step])
                lines.append(total)
        high, low = split(jnp.concatenate(lines, axis=0))
        both = jnp.dot(
            jnp.concatenate([high, low], axis=1), column_table[channel], preferred_element_type=f32
        )
        smooth = both[:, :NX] + both[:, NX:]
        features[channel] = jnp.log(1.0 + smooth)
        return carry

    lax.fori_loop(0, CHAN, channel_step, 0, unroll=8)

    def cell_step(step, carry):
        start = pl.multiple_of(step * 16, 16)
        inputs = [features[channel, pl.ds(start, 16), :] for channel in range(CHAN)]
        cells = jnp.concatenate(
            [
                jnp.concatenate([piece[:8] for piece in inputs], axis=0),
                jnp.concatenate([piece[8:] for piece in inputs], axis=0),
            ],
            axis=1,
        )
        high, low = split(cells)
        ones = jnp.ones((16, 2 * NX), bf16)
        stacked = jnp.concatenate([high, low, high, ones], axis=0)
        values = []
        for half in range(2):
            hidden = jnp.dot(
                first_table[256 * half : 256 * half + 256, :], stacked, preferred_element_type=f32
            )
            hidden = hidden + hidden * jnp.tanh(hidden)
            hidden_high, hidden_low = split(hidden)
            for pair in range(2):
                rows = slice(128 * pair, 128 * pair + 128)
                both = jnp.dot(
                    middle_table[...],
                    jnp.concatenate([hidden_high[rows], hidden_low[rows]], axis=0),
                    preferred_element_type=f32,
                )
                mixed = both[:128] + both[128:] + middle_bias[...]
                mixed = (mixed + mixed * jnp.tanh(mixed)) * last_weight[...]
                values.append(jnp.sum(mixed.reshape(2, HID, 2 * NX), axis=1))
        value = jnp.concatenate(values, axis=0) + last_bias[0]
        result[pl.ds(start, 8), :] = value[:, :NX]
        result[pl.ds(start + 8, 8), :] = value[:, NX:]
        return carry

    lax.fori_loop(0, CZ * HALF // 16, cell_step, 0, unroll=9)
    for part in range(CZ // 8):
        block = result[HALF * 8 * part : HALF * 8 * (part + 1), :]
        planes[:HALF, 8 * part : 8 * part + 8, :] = block.reshape(HALF, 8, NX)
    potential[...] = planes[:HALF, :CZ, :].astype(bf16)


def model(kept, other, taps, tables):
    return pl.pallas_call(
        model_body,
        name="smooth_and_network",
        out_shape=jax.ShapeDtypeStruct((HALF, CZ, NX), bf16),
        in_specs=[SMEM] + [VMEM] * 8 + [SMEM],
        out_specs=VMEM,
        scratch_shapes=[
            pltpu.VMEM((ROWS, CHAN * CZ, NX), f32),
            pltpu.VMEM((CHAN, HALF * CZ, NX), f32),
            pltpu.VMEM((HALF * CZ, NX), f32),
            pltpu.VMEM((ROWS * DEPTH, NX), f32),
        ],
        compiler_params=ROOM,
    )(taps, kept, other, *tables)


def tap_weights(kernel_widths, distance):
    width = kernel_widths.reshape((CHAN,) + (1,) * distance.ndim)
    reach = jnp.arange(-RAD, RAD + 1).astype(f32).reshape((2 * RAD + 1,) + (1,) * distance.ndim)
    whole = jnp.sum(jnp.exp(-(reach**2)[None] / (2.0 * width[:, None] ** 2)), axis=1)
    far = distance.astype(f32)[None]
    raw = jnp.where(jnp.abs(far) <= RAD, jnp.exp(-(far**2) / (2.0 * width**2)), 0.0)
    return raw / whole


def model_tables(kernel_widths, w_in, b_in, w_mid, b_mid, w_out, b_out):
    out_index = jnp.arange(CZ, dtype=jnp.int32)
    in_index = jnp.arange(DEPTH, dtype=jnp.int32) - RAD
    plane = tap_weights(kernel_widths, in_index[None, :] - out_index[:, None])
    plane = plane.reshape(CHAN * CZ, DEPTH)
    plane_table = jnp.concatenate(split_table(plane), axis=0)
    source = jnp.arange(NX, dtype=jnp.int32)
    around = (source[:, None] - source[None, :] + NX // 2) % NX - NX // 2
    column = tap_weights(kernel_widths, around)
    column_high, column_low = split_table(column)
    column_table = jnp.concatenate(
        [
            jnp.concatenate([column_high, column_low], axis=2),
            jnp.concatenate([column_high, jnp.zeros_like(column_low)], axis=2),
        ],
        axis=1,
    )
    eight = jnp.eye(8, dtype=f32)
    first = (0.5 * w_in.T)[None, :, :, None] * eight[:, None, None, :]
    first_high, first_low = split_table(first.reshape(8 * HID, CHAN * 8))
    bias_high, bias_low = split_table(jnp.tile(0.5 * b_in, 8)[:, None])
    first_table = jnp.concatenate(
        [
            first_high,
            first_high,
            first_low,
            bias_high,
            bias_low,
            jnp.zeros((8 * HID, 14), bf16),
        ],
        axis=1,
    )
    two = jnp.eye(2, dtype=f32)
    middle = (two[:, None, :, None] * (0.5 * w_mid.T)[None, :, None, :]).reshape(2 * HID, 2 * HID)
    middle_high, middle_low = split_table(middle)
    middle_table = jnp.concatenate(
        [
            jnp.concatenate([middle_high, middle_high], axis=1),
            jnp.concatenate([middle_low, jnp.zeros_like(middle_low)], axis=1),
        ],
        axis=0,
    )
    middle_bias = jnp.broadcast_to(jnp.tile(0.5 * b_mid, 2)[:, None], (2 * HID, 2 * NX))
    last_weight = jnp.broadcast_to(jnp.tile(w_out, 2)[:, None], (2 * HID, 2 * NX))
    return (
        plane_table,
        column_table,
        first_table,
        middle_table,
        middle_bias,
        last_weight,
        b_out,
    )


def widen_body(position, far, near, partner, own, wide, first_planes, last_planes):
    orb = position[0]
    wide[pl.ds(HALF + HALF * orb, HALF)] = own[...]
    wide[pl.ds(2 * HALF - HALF * orb, HALF)] = partner[...]
    wide[pl.ds(3 * HALF * orb, HALF)] = near[...]
    wide[pl.ds(3 * HALF - 3 * HALF * orb, HALF)] = far[...]
    first_planes[...] = wide[:, :16, :]
    last_planes[...] = wide[...].astype(f32)[:, CZ - 16 :, :].astype(bf16)


def widen(position, far, near, partner, own):
    return pl.pallas_call(
        widen_body,
        name="widen_rows",
        out_shape=(
            jax.ShapeDtypeStruct((CY + BOX, CZ, NX), bf16),
            jax.ShapeDtypeStruct((CY + BOX, 16, NX), bf16),
            jax.ShapeDtypeStruct((CY + BOX, 16, NX), bf16),
        ),
        in_specs=[SMEM] + [VMEM] * 4,
        out_specs=(VMEM,) * 3,
        compiler_params=ROOM,
    )(position, far, near, partner, own)


def cut_body(rows, wide, below, above, windows, reach, cuts, offsets, offsets_sem, sems):
    fetch = pltpu.make_async_copy(rows, offsets, offsets_sem)
    fetch.start()
    reach[:, :16, :] = below[...].astype(f32)
    reach[:, 16 : 16 + CZ, :] = wide[...].astype(f32)
    reach[:, 16 + CZ :, :] = above[...].astype(f32)
    fetch.wait()
    lane = lanes(BOX)

    def source_step(source, carry):
        mains, tails = [], []
        for slot in range(CAP):
            z0 = offsets[source, 64 * slot] + 16 - FIRST_PLANE
            y0 = offsets[source, 64 * slot + 1]
            x0 = offsets[source, 64 * slot + 2]
            tiles = [None] * 5
            for b in range(BOX):
                tile, left = divmod(BOX * b, NX)
                piece = reach[y0 + b, pl.ds(z0, BOX), :]
                piece = pltpu.roll(piece, (left - x0) & (NX - 1), 1)
                if tiles[tile] is None:
                    tiles[tile] = piece
                else:
                    tiles[tile] = jnp.where(lane >= left, piece, tiles[tile])
                if left + BOX > NX:
                    tiles[tile + 1] = piece
            mains += tiles[:4]
            tails.append(tiles[4])
        tail = jnp.where(lane < 64, tails[0], pltpu.roll(tails[1], 64, 1))
        cuts[source] = jnp.concatenate(mains + [tail], axis=0).astype(bf16)
        return carry

    copies = []
    for first in range(0, SLABS, PART):
        lax.fori_loop(first, first + PART, source_step, 0, unroll=4)
        copy = pltpu.make_async_copy(
            cuts.at[pl.ds(first, PART)], windows.at[pl.ds(first, PART)], sems.at[first // PART]
        )
        copy.start()
        copies.append(copy)
    for copy in copies:
        copy.wait()


def cut(offsets, wide, below, above):
    return pl.pallas_call(
        cut_body,
        name="cut_windows",
        out_shape=jax.ShapeDtypeStruct((SLABS, WINDOW_ROWS, NX), bf16),
        in_specs=[VMEM] * 4,
        out_specs=pl.BlockSpec(memory_space=pl.ANY),
        scratch_shapes=[
            pltpu.VMEM((CY + BOX, CZ + 32, NX), f32),
            pltpu.VMEM((SLABS, WINDOW_ROWS, NX), bf16),
            pltpu.SMEM((SLABS, NX), jnp.int32),
            pltpu.SemaphoreType.DMA,
            pltpu.SemaphoreType.DMA((SLABS // PART,)),
        ],
        compiler_params=ROOM,
    )(offsets, wide, below, above)


def apply_body(corners, windows, orbitals, applied, products, count, sems):
    def clear(slab, carry):
        count[slab] = 0
        return carry

    lax.fori_loop(0, SLABS, clear, 0)

    def place(i, carry):
        slab = lax.div(corners[0, i], CZ)
        rank = count[slab]
        count[slab] = rank + 1
        main = windows[slab, pl.ds(pl.multiple_of(rank * MAIN, 32), MAIN), :].astype(f32)
        tail = windows[slab, TAIL:WINDOW_ROWS, :].astype(f32)
        tail = jnp.where(rank == 0, tail[:, :64], tail[:, 64:])
        whole = jnp.concatenate([main[BOX * j : BOX * j + BOX] for j in range(4)] + [tail], axis=1)
        products[i] = (whole * orbitals[i].astype(f32)).astype(bf16)
        return carry

    copies = []
    for first in range(0, HELD, PART):
        lax.fori_loop(first, first + PART, place, 0, unroll=4)
        copy = pltpu.make_async_copy(
            products.at[pl.ds(first, PART)], applied.at[pl.ds(first, PART)], sems.at[first // PART]
        )
        copy.start()
        copies.append(copy)
    for copy in copies:
        copy.wait()


def apply(corners, windows, orbitals):
    return pl.pallas_call(
        apply_body,
        name="apply_windows",
        out_shape=jax.ShapeDtypeStruct(orbitals.shape, bf16),
        in_specs=[SMEM, VMEM, VMEM],
        out_specs=pl.BlockSpec(memory_space=pl.ANY),
        scratch_shapes=[
            pltpu.VMEM((HELD, BOX, BOX * BOX), bf16),
            pltpu.SMEM((SLABS,), jnp.int32),
            pltpu.SemaphoreType.DMA((HELD // PART,)),
        ],
        compiler_params=ROOM,
    )(corners, windows, orbitals)


def exchange(x, axis):
    return lax.all_to_all(x, axis, split_axis=0, concat_axis=0, tiled=True)


def local(orbitals, occupation, corners, kernel_widths, w_in, b_in, w_mid, b_mid, w_out, b_out):
    corners = corners.T
    taps = tap_weights(kernel_widths, jnp.arange(-RAD, RAD + 1))
    tables = model_tables(kernel_widths, w_in, b_in, w_mid, b_mid, w_out, b_out)
    received = exchange(pack(corners, occupation, orbitals), "gz")
    received, taps, tables = lax.optimization_barrier((received, taps, tables))
    position = lax.axis_index("orb").reshape(1)
    own, next_up, next_down, offsets = deposit(received)
    kept, next_right, next_left = fold_planes(
        own, shifted(next_up, "gz", 1), shifted(next_down, "gz", -1)
    )
    left = across_rows(next_right, (1, 1), 1)
    right = across_rows(next_left, (-1, -1), 1)
    kept, given = fold_rows(position, kept, left, right)
    half = model(kept, shifted(given, "orb", 1), taps, tables)
    far = across_rows(half, (-1, 1), 0)
    near = across_rows(half, (-1, 1), 1)
    partner = shifted(half, "orb", 1)
    wide, first_planes, last_planes = widen(position, far, near, partner, half)
    below = shifted(last_planes, "gz", 1)
    above = shifted(first_planes, "gz", -1)
    windows = cut(offsets, wide, below, above)
    applied = apply(corners, exchange(windows, "gz"), orbitals)
    tile = jnp.concatenate([below[:CY, 16 - FIRST_PLANE :], wide[:CY, : CZ - FIRST_PLANE]], axis=1)
    return jnp.transpose(tile, (1, 0, 2)), applied


def solution(mesh):
    return jax.shard_map(
        local,
        mesh=mesh,
        in_specs=(
            P(("gz", "gy", "orb"), None, None),
            P(("gz", "gy", "orb")),
            P(("gz", "gy", "orb"), None),
            P(),
            P(),
            P(),
            P(),
            P(),
            P(),
            P(),
        ),
        out_specs=(P("gz", "gy", None), P(("gz", "gy", "orb"), None, None)),
        check_vma=False,
    )
```

```python
import jax
import jax.numpy as jnp
from jax import lax
from jax.experimental import pallas as pl
from jax.experimental.pallas import tpu as pltpu
from jax.sharding import PartitionSpec as P

BOX = 24
CHAN = 8
HID = 64
RAD = 6
CZ = 24
CY = 24
NX = 128
CAP = 2
SLABS = 16
HELD = 16
FIRST_PLANE = 10
PLANES = 40
SKIP = FIRST_PLANE - RAD
DEPTH = PLANES - SKIP
ABOVE = PLANES - CZ
HALF = CY // 2
ROWS = HALF + 2 * RAD
REACH = CY + 2 * RAD
EDGE = REACH // 2
MAIN = 96
TAIL = CAP * MAIN
BLOCK_ROWS = 224
GROUP = 4
PART = 4
WINDOW_ROWS = TAIL + BOX

VMEM = pl.BlockSpec(memory_space=pltpu.VMEM)
SMEM = pl.BlockSpec(memory_space=pltpu.SMEM)
ROOM = pltpu.CompilerParams(vmem_limit_bytes=16 * 1024 * 1024)
f32 = jnp.float32
bf16 = jnp.bfloat16


def shifted(x, axis, by):
    count = lax.axis_size(axis)
    return lax.ppermute(x, axis, [(i, (i + by) % count) for i in range(count)])


def across_rows(x, steps, cross):
    tiles, owners = lax.axis_size("gy"), lax.axis_size("orb")
    pairs = [
        (tile * owners + orb, (tile + steps[orb]) % tiles * owners + (orb + cross) % owners)
        for tile in range(tiles)
        for orb in range(owners)
    ]
    return lax.ppermute(x, ("gy", "orb"), pairs)


def split(x):
    high = x.astype(bf16)
    return high, (x - high.astype(f32)).astype(bf16)


def split_table(x):
    high = lax.reduce_precision(x, 8, 7)
    return high.astype(bf16), (x - high).astype(bf16)


def lanes(rows):
    return lax.broadcasted_iota(jnp.int32, (rows, NX), 1)


def pack_body(corners_in, occupation_in, orbitals, sent, boxes, corners, occupation, count, scalar_sems, sems):
    scalars = [
        pltpu.make_async_copy(corners_in, corners, scalar_sems.at[0]),
        pltpu.make_async_copy(occupation_in, occupation, scalar_sems.at[1]),
    ]
    for copy in scalars:
        copy.start()
    copies = [
        pltpu.make_async_copy(
            orbitals.at[pl.ds(PART * i, PART)], boxes.at[pl.ds(PART * i, PART)], sems.at[i]
        )
        for i in range(HELD // PART)
    ]
    for copy in copies:
        copy.start()
    sent[...] = jnp.zeros(sent.shape, bf16)

    def clear(slab, carry):
        count[slab] = 0
        return carry

    lax.fori_loop(0, SLABS, clear, 0)
    side = lanes(32) // 64
    field = lanes(8) % 64

    def place(i):
        plane = corners[0, i]
        row = corners[1, i]
        column = corners[2, i]
        slab = lax.div(plane, CZ)
        rank = count[slab]
        count[slab] = rank + 1
        values = boxes[i].astype(f32)
        density = occupation[i] * values * values
        main = jnp.concatenate([density[:, 128 * j : 128 * j + 128] for j in range(4)], axis=0)
        sent[slab, pl.ds(pl.multiple_of(rank * MAIN, 32), MAIN), :] = main.astype(bf16)
        last = density[:, 512:576]
        tail = jnp.concatenate([last, last], axis=1)
        offsets = jnp.where(
            field == 0,
            lax.rem(plane, CZ),
            jnp.where(field == 1, lax.rem(row, CY), jnp.where(field == 2, column, 0)),
        ).astype(f32)
        fresh = jnp.concatenate([tail, offsets], axis=0)
        held = sent[slab, TAIL:BLOCK_ROWS, :].astype(f32)
        sent[slab, TAIL:BLOCK_ROWS, :] = jnp.where(side == rank, fresh, held).astype(bf16)

    for copy in scalars:
        copy.wait()
    for i in range(HELD):
        if i % PART == 0:
            copies[i // PART].wait()
        place(i)


def pack(corners, occupation, orbitals):
    return pl.pallas_call(
        pack_body,
        name="pack_boxes",
        out_shape=jax.ShapeDtypeStruct((SLABS, BLOCK_ROWS, NX), bf16),
        in_specs=[pl.BlockSpec(memory_space=pl.ANY)] * 3,
        out_specs=VMEM,
        scratch_shapes=[
            pltpu.VMEM((HELD, BOX, BOX * BOX), bf16),
            pltpu.SMEM((3, HELD), jnp.int32),
            pltpu.SMEM((HELD,), f32),
            pltpu.SMEM((SLABS,), jnp.int32),
            pltpu.SemaphoreType.DMA((2,)),
            pltpu.SemaphoreType.DMA((HELD // PART,)),
        ],
        compiler_params=pltpu.CompilerParams(vmem_limit_bytes=60 * 1024 * 1024),
    )(corners, occupation, orbitals)


def read_offsets(received, rows, offsets, sem):
    for source in range(SLABS):
        rows[source : source + 1, :] = (
            received[source, 208:BLOCK_ROWS, :].astype(f32)[8:9].astype(jnp.int32)
        )
    copy = pltpu.make_async_copy(rows, offsets, sem)
    copy.start()
    return copy


def deposit_body(received, own, next_up, next_down, offsets_out, grids, rows, offsets, sem):
    copy = read_offsets(received, rows, offsets, sem)
    offsets_out[...] = rows[...]
    for grid in grids:
        grid[...] = jnp.zeros(grid.shape, f32)
    copy.wait()
    lane = lanes(BOX)

    def source_step(source, carry):
        tail_both = received[source, TAIL:BLOCK_ROWS, :].astype(f32)[:BOX]
        boxes = []
        for slot in range(CAP):
            start = [offsets[source, 64 * slot + field] for field in range(3)]
            main = received[source, MAIN * slot : MAIN * slot + MAIN, :].astype(f32)
            tiles = [main[BOX * j : BOX * j + BOX] for j in range(4)]
            tiles.append(tail_both if slot == 0 else pltpu.roll(tail_both, 64, 1))
            boxes.append((start, tiles, ((lane - start[2]) & (NX - 1)) < BOX))
        for first in range(0, BOX, GROUP):
            for slot in range(CAP):
                (z0, y0, x0), tiles, inside = boxes[slot]
                grid = grids[slot]
                olds = [grid[y0 + first + k, pl.ds(z0, BOX), :] for k in range(GROUP)]
                news = []
                for k in range(GROUP):
                    tile, left = divmod(BOX * (first + k), NX)
                    piece = tiles[tile]
                    if left + BOX > NX:
                        piece = jnp.where(lane >= left, piece, tiles[tile + 1])
                    piece = pltpu.roll(piece, (x0 - left) & (NX - 1), 1)
                    news.append(olds[k] + jnp.where(inside, piece, 0.0))
                for k in range(GROUP):
                    grid[y0 + first + k, pl.ds(z0, BOX), :] = news[k]
        return carry

    lax.fori_loop(0, SLABS, source_step, 0, unroll=2)
    own[...] = grids[0][:, :PLANES, :] + grids[1][:, :PLANES, :]
    next_up[...] = (grids[0][:, CZ:, :] + grids[1][:, CZ:, :]).astype(bf16)
    next_down[...] = (grids[0][:, :ABOVE, :] + grids[1][:, :ABOVE, :]).astype(bf16)


def deposit(received):
    return pl.pallas_call(
        deposit_body,
        name="deposit_boxes",
        out_shape=(
            jax.ShapeDtypeStruct((CY + BOX, PLANES, NX), f32),
            jax.ShapeDtypeStruct((CY + BOX, BOX, NX), bf16),
            jax.ShapeDtypeStruct((CY + BOX, ABOVE, NX), bf16),
            jax.ShapeDtypeStruct((SLABS, NX), jnp.int32),
        ),
        in_specs=[VMEM],
        out_specs=(VMEM,) * 4,
        scratch_shapes=[
            [pltpu.VMEM((CY + BOX, CZ + BOX, NX), f32)] * CAP,
            pltpu.VMEM((SLABS, NX), jnp.int32),
            pltpu.SMEM((SLABS, NX), jnp.int32),
            pltpu.SemaphoreType.DMA,
        ],
        compiler_params=ROOM,
    )(received)


def fold_planes_body(own, below, above, kept, next_right, next_left, total, flat):
    total[:, :CZ, :] = own[:, :CZ, :] + below[...].astype(f32)
    total[:, CZ:, :] = own[:, CZ:, :] + above[...].astype(f32)
    kept[...] = total[RAD : RAD + REACH, SKIP:, :]
    for side, first, sent in ((0, 2 * CY - EDGE, next_right), (1, 0, next_left)):
        for row in range(EDGE):
            flat[side, DEPTH * row : DEPTH * (row + 1), :] = total[first + row, SKIP:, :]
        sent[...] = flat[side].astype(bf16)


def fold_planes(own, below, above):
    return pl.pallas_call(
        fold_planes_body,
        name="fold_planes",
        out_shape=(
            jax.ShapeDtypeStruct((REACH, DEPTH, NX), f32),
            jax.ShapeDtypeStruct((EDGE * DEPTH, NX), bf16),
            jax.ShapeDtypeStruct((EDGE * DEPTH, NX), bf16),
        ),
        in_specs=[VMEM] * 3,
        out_specs=(VMEM,) * 3,
        scratch_shapes=[
            pltpu.VMEM((CY + BOX, PLANES, NX), f32),
            pltpu.VMEM((2, EDGE * DEPTH, NX), f32),
        ],
        compiler_params=ROOM,
    )(own, below, above)


def fold_rows_body(position, own, left, right, kept, given, total, sides, flat):
    for side, received in enumerate((left, right)):
        sides[side] = received[...].astype(f32)
        for row in range(EDGE):
            total[EDGE * side + row] = (
                own[EDGE * side + row] + sides[side, DEPTH * row : DEPTH * (row + 1), :]
            )
    orb = position[0]
    kept[...] = total[pl.ds(HALF * orb, ROWS)]
    for row in range(ROWS):
        flat[DEPTH * row : DEPTH * (row + 1), :] = total[HALF * (1 - orb) + row]
    given[...] = flat[...].astype(bf16)


def fold_rows(position, own, left, right):
    return pl.pallas_call(
        fold_rows_body,
        name="fold_rows",
        out_shape=(
            jax.ShapeDtypeStruct((ROWS, DEPTH, NX), f32),
            jax.ShapeDtypeStruct((ROWS * DEPTH, NX), bf16),
        ),
        in_specs=[SMEM] + [VMEM] * 3,
        out_specs=(VMEM, VMEM),
        scratch_shapes=[
            pltpu.VMEM((REACH, DEPTH, NX), f32),
            pltpu.VMEM((2, EDGE * DEPTH, NX), f32),
            pltpu.VMEM((ROWS * DEPTH, NX), f32),
        ],
        compiler_params=ROOM,
    )(position, own, left, right)


def model_body(
    taps,
    kept,
    other,
    plane_table,
    column_table,
    first_table,
    middle_table,
    middle_bias,
    last_weight,
    last_bias,
    potential,
    planes,
    features,
    result,
    flat,
):
    flat[...] = other[...].astype(f32)

    def plane_step(pair, carry):
        density = [
            kept[row] + flat[pl.ds(DEPTH * row, DEPTH), :] for row in (2 * pair, 2 * pair + 1)
        ]
        field = jnp.concatenate(density, axis=1).astype(bf16)
        both = jnp.dot(plane_table[...], field, preferred_element_type=f32)
        total = both[: CHAN * CZ] + both[CHAN * CZ :]
        planes[2 * pair] = total[:, :NX]
        planes[2 * pair + 1] = total[:, NX:]
        return carry

    lax.fori_loop(0, ROWS // 2, plane_step, 0, unroll=12)

    def channel_step(channel, carry):
        weights = [taps[channel, step] for step in range(RAD + 1)]
        lines = []
        for part in range(CZ // 8):
            start = pl.multiple_of(channel * CZ + 8 * part, 8)
            rows = [planes[y, pl.ds(start, 8), :] for y in range(ROWS)]
            for y in range(HALF):
                total = weights[RAD] * rows[y + RAD]
                for step in range(RAD):
                    total = total + weights[step] * (rows[y + step] + rows[y + 2 * RAD - step])
                lines.append(total)
        high, low = split(jnp.concatenate(lines, axis=0))
        both = jnp.dot(
            jnp.concatenate([high, low], axis=1), column_table[channel], preferred_element_type=f32
        )
        smooth = both[:, :NX] + both[:, NX:]
        features[channel] = jnp.log(1.0 + smooth)
        return carry

    lax.fori_loop(0, CHAN, channel_step, 0, unroll=8)

    def cell_step(step, carry):
        start = pl.multiple_of(step * 16, 16)
        inputs = [features[channel, pl.ds(start, 16), :] for channel in range(CHAN)]
        cells = jnp.concatenate(
            [
                jnp.concatenate([piece[:8] for piece in inputs], axis=0),
                jnp.concatenate([piece[8:] for piece in inputs], axis=0),
            ],
            axis=1,
        )
        high, low = split(cells)
        ones = jnp.ones((16, 2 * NX), bf16)
        stacked = jnp.concatenate([high, low, high, ones], axis=0)
        values = []
        for half in range(2):
            hidden = jnp.dot(
                first_table[256 * half : 256 * half + 256, :], stacked, preferred_element_type=f32
            )
            hidden = hidden + hidden * jnp.tanh(hidden)
            hidden_high, hidden_low = split(hidden)
            for pair in range(2):
                rows = slice(128 * pair, 128 * pair + 128)
                both = jnp.dot(
                    middle_table[...],
                    jnp.concatenate([hidden_high[rows], hidden_low[rows]], axis=0),
                    preferred_element_type=f32,
                )
                mixed = both[:128] + both[128:] + middle_bias[...]
                mixed = (mixed + mixed * jnp.tanh(mixed)) * last_weight[...]
                values.append(jnp.sum(mixed.reshape(2, HID, 2 * NX), axis=1))
        value = jnp.concatenate(values, axis=0) + last_bias[0]
        result[pl.ds(start, 8), :] = value[:, :NX]
        result[pl.ds(start + 8, 8), :] = value[:, NX:]
        return carry

    lax.fori_loop(0, CZ * HALF // 16, cell_step, 0, unroll=9)
    for part in range(CZ // 8):
        block = result[HALF * 8 * part : HALF * 8 * (part + 1), :]
        planes[:HALF, 8 * part : 8 * part + 8, :] = block.reshape(HALF, 8, NX)
    potential[...] = planes[:HALF, :CZ, :].astype(bf16)


def model(kept, other, taps, tables):
    return pl.pallas_call(
        model_body,
        name="smooth_and_network",
        out_shape=jax.ShapeDtypeStruct((HALF, CZ, NX), bf16),
        in_specs=[SMEM] + [VMEM] * 8 + [SMEM],
        out_specs=VMEM,
        scratch_shapes=[
            pltpu.VMEM((ROWS, CHAN * CZ, NX), f32),
            pltpu.VMEM((CHAN, HALF * CZ, NX), f32),
            pltpu.VMEM((HALF * CZ, NX), f32),
            pltpu.VMEM((ROWS * DEPTH, NX), f32),
        ],
        compiler_params=ROOM,
    )(taps, kept, other, *tables)


def tap_weights(kernel_widths, distance):
    width = kernel_widths.reshape((CHAN,) + (1,) * distance.ndim)
    reach = jnp.arange(-RAD, RAD + 1).astype(f32).reshape((2 * RAD + 1,) + (1,) * distance.ndim)
    whole = jnp.sum(jnp.exp(-(reach**2)[None] / (2.0 * width[:, None] ** 2)), axis=1)
    far = distance.astype(f32)[None]
    raw = jnp.where(jnp.abs(far) <= RAD, jnp.exp(-(far**2) / (2.0 * width**2)), 0.0)
    return raw / whole


def model_tables(kernel_widths, w_in, b_in, w_mid, b_mid, w_out, b_out):
    out_index = jnp.arange(CZ, dtype=jnp.int32)
    in_index = jnp.arange(DEPTH, dtype=jnp.int32) - RAD
    plane = tap_weights(kernel_widths, in_index[None, :] - out_index[:, None])
    plane = plane.reshape(CHAN * CZ, DEPTH)
    plane_table = jnp.concatenate(split_table(plane), axis=0)
    source = jnp.arange(NX, dtype=jnp.int32)
    around = (source[:, None] - source[None, :] + NX // 2) % NX - NX // 2
    column = tap_weights(kernel_widths, around)
    column_high, column_low = split_table(column)
    column_table = jnp.concatenate(
        [
            jnp.concatenate([column_high, column_low], axis=2),
            jnp.concatenate([column_high, jnp.zeros_like(column_low)], axis=2),
        ],
        axis=1,
    )
    eight = jnp.eye(8, dtype=f32)
    first = (0.5 * w_in.T)[None, :, :, None] * eight[:, None, None, :]
    first_high, first_low = split_table(first.reshape(8 * HID, CHAN * 8))
    bias_high, bias_low = split_table(jnp.tile(0.5 * b_in, 8)[:, None])
    first_table = jnp.concatenate(
        [
            first_high,
            first_high,
            first_low,
            bias_high,
            bias_low,
            jnp.zeros((8 * HID, 14), bf16),
        ],
        axis=1,
    )
    two = jnp.eye(2, dtype=f32)
    middle = (two[:, None, :, None] * (0.5 * w_mid.T)[None, :, None, :]).reshape(2 * HID, 2 * HID)
    middle_high, middle_low = split_table(middle)
    middle_table = jnp.concatenate(
        [
            jnp.concatenate([middle_high, middle_high], axis=1),
            jnp.concatenate([middle_low, jnp.zeros_like(middle_low)], axis=1),
        ],
        axis=0,
    )
    middle_bias = jnp.broadcast_to(jnp.tile(0.5 * b_mid, 2)[:, None], (2 * HID, 2 * NX))
    last_weight = jnp.broadcast_to(jnp.tile(w_out, 2)[:, None], (2 * HID, 2 * NX))
    return (
        plane_table,
        column_table,
        first_table,
        middle_table,
        middle_bias,
        last_weight,
        b_out,
    )


def widen_body(position, near, far, partner, own, wide, first_planes, last_planes):
    orb = position[0]
    wide[pl.ds(HALF + HALF * orb, HALF)] = own[...]
    wide[pl.ds(2 * HALF - HALF * orb, HALF)] = partner[...]
    wide[pl.ds(3 * HALF * orb, HALF)] = near[...]
    wide[pl.ds(3 * HALF - 3 * HALF * orb, HALF)] = far[...]
    first_planes[...] = wide[:, :16, :]
    last_planes[...] = wide[...].astype(f32)[:, CZ - 16 :, :].astype(bf16)


def widen(position, near, far, partner, own):
    return pl.pallas_call(
        widen_body,
        name="widen_rows",
        out_shape=(
            jax.ShapeDtypeStruct((CY + BOX, CZ, NX), bf16),
            jax.ShapeDtypeStruct((CY + BOX, 16, NX), bf16),
            jax.ShapeDtypeStruct((CY + BOX, 16, NX), bf16),
        ),
        in_specs=[SMEM] + [VMEM] * 4,
        out_specs=(VMEM,) * 3,
        compiler_params=ROOM,
    )(position, near, far, partner, own)


def cut_body(rows, wide, below, above, windows, reach, cuts, offsets, offsets_sem, sems):
    fetch = pltpu.make_async_copy(rows, offsets, offsets_sem)
    fetch.start()
    reach[:, :16, :] = below[...].astype(f32)
    reach[:, 16 : 16 + CZ, :] = wide[...].astype(f32)
    reach[:, 16 + CZ :, :] = above[...].astype(f32)
    fetch.wait()
    lane = lanes(BOX)

    def source_step(source, carry):
        mains, tails = [], []
        for slot in range(CAP):
            z0 = offsets[source, 64 * slot] + 16 - FIRST_PLANE
            y0 = offsets[source, 64 * slot + 1]
            x0 = offsets[source, 64 * slot + 2]
            tiles = [None] * 5
            for b in range(BOX):
                tile, left = divmod(BOX * b, NX)
                piece = reach[y0 + b, pl.ds(z0, BOX), :]
                piece = pltpu.roll(piece, (left - x0) & (NX - 1), 1)
                if tiles[tile] is None:
                    tiles[tile] = piece
                else:
                    tiles[tile] = jnp.where(lane >= left, piece, tiles[tile])
                if left + BOX > NX:
                    tiles[tile + 1] = piece
            mains += tiles[:4]
            tails.append(tiles[4])
        tail = jnp.where(lane < 64, tails[0], pltpu.roll(tails[1], 64, 1))
        cuts[source] = jnp.concatenate(mains + [tail], axis=0).astype(bf16)
        return carry

    copies = []
    for first in range(0, SLABS, PART):
        lax.fori_loop(first, first + PART, source_step, 0, unroll=4)
        copy = pltpu.make_async_copy(
            cuts.at[pl.ds(first, PART)], windows.at[pl.ds(first, PART)], sems.at[first // PART]
        )
        copy.start()
        copies.append(copy)
    for copy in copies:
        copy.wait()


def cut(offsets, wide, below, above):
    return pl.pallas_call(
        cut_body,
        name="cut_windows",
        out_shape=jax.ShapeDtypeStruct((SLABS, WINDOW_ROWS, NX), bf16),
        in_specs=[VMEM] * 4,
        out_specs=pl.BlockSpec(memory_space=pl.ANY),
        scratch_shapes=[
            pltpu.VMEM((CY + BOX, CZ + 32, NX), f32),
            pltpu.VMEM((SLABS, WINDOW_ROWS, NX), bf16),
            pltpu.SMEM((SLABS, NX), jnp.int32),
            pltpu.SemaphoreType.DMA,
            pltpu.SemaphoreType.DMA((SLABS // PART,)),
        ],
        compiler_params=ROOM,
    )(offsets, wide, below, above)


def apply_body(corners, windows, orbitals, applied, products, count, sems):
    def clear(slab, carry):
        count[slab] = 0
        return carry

    lax.fori_loop(0, SLABS, clear, 0)

    def place(i, carry):
        slab = lax.div(corners[0, i], CZ)
        rank = count[slab]
        count[slab] = rank + 1
        main = windows[slab, pl.ds(pl.multiple_of(rank * MAIN, 32), MAIN), :].astype(f32)
        tail = windows[slab, TAIL:WINDOW_ROWS, :].astype(f32)
        tail = jnp.where(rank == 0, tail[:, :64], tail[:, 64:])
        whole = jnp.concatenate([main[BOX * j : BOX * j + BOX] for j in range(4)] + [tail], axis=1)
        products[i] = (whole * orbitals[i].astype(f32)).astype(bf16)
        return carry

    copies = []
    for first in range(0, HELD, PART):
        lax.fori_loop(first, first + PART, place, 0, unroll=4)
        copy = pltpu.make_async_copy(
            products.at[pl.ds(first, PART)], applied.at[pl.ds(first, PART)], sems.at[first // PART]
        )
        copy.start()
        copies.append(copy)
    for copy in copies:
        copy.wait()


def apply(corners, windows, orbitals):
    return pl.pallas_call(
        apply_body,
        name="apply_windows",
        out_shape=jax.ShapeDtypeStruct(orbitals.shape, bf16),
        in_specs=[SMEM, VMEM, VMEM],
        out_specs=pl.BlockSpec(memory_space=pl.ANY),
        scratch_shapes=[
            pltpu.VMEM((HELD, BOX, BOX * BOX), bf16),
            pltpu.SMEM((SLABS,), jnp.int32),
            pltpu.SemaphoreType.DMA((HELD // PART,)),
        ],
        compiler_params=ROOM,
    )(corners, windows, orbitals)


def exchange(x, axis):
    return lax.all_to_all(x, axis, split_axis=0, concat_axis=0, tiled=True)


def local(orbitals, occupation, corners, kernel_widths, w_in, b_in, w_mid, b_mid, w_out, b_out):
    corners = corners.T
    taps = tap_weights(kernel_widths, jnp.arange(-RAD, RAD + 1))
    tables = model_tables(kernel_widths, w_in, b_in, w_mid, b_mid, w_out, b_out)
    received = exchange(pack(corners, occupation, orbitals), "gz")
    received, taps, tables = lax.optimization_barrier((received, taps, tables))
    position = lax.axis_index("orb").reshape(1)
    own, next_up, next_down, offsets = deposit(received)
    kept, next_right, next_left = fold_planes(
        own, shifted(next_up, "gz", 1), shifted(next_down, "gz", -1)
    )
    left = across_rows(next_right, (1, 1), 1)
    right = across_rows(next_left, (-1, -1), 1)
    kept, given = fold_rows(position, kept, left, right)
    half = model(kept, shifted(given, "orb", 1), taps, tables)
    far = across_rows(half, (-1, 1), 0)
    near = across_rows(half, (-1, 1), 1)
    partner = shifted(half, "orb", 1)
    wide, first_planes, last_planes = widen(position, near, far, partner, half)
    below = shifted(last_planes, "gz", 1)
    above = shifted(first_planes, "gz", -1)
    windows = cut(offsets, wide, below, above)
    applied = apply(corners, exchange(windows, "gz"), orbitals)
    tile = jnp.concatenate([below[:CY, 16 - FIRST_PLANE :], wide[:CY, : CZ - FIRST_PLANE]], axis=1)
    return jnp.transpose(tile, (1, 0, 2)), applied


def solution(mesh):
    return jax.shard_map(
        local,
        mesh=mesh,
        in_specs=(
            P(("gz", "gy", "orb"), None, None),
            P(("gz", "gy", "orb")),
            P(("gz", "gy", "orb"), None),
            P(),
            P(),
            P(),
            P(),
            P(),
            P(),
            P(),
        ),
        out_specs=(P("gz", "gy", None), P(("gz", "gy", "orb"), None, None)),
        check_vma=False,
    )
```
